32 devices in a mesh: row: 4 (over y, x), col: 8 (over z, core).
Axes of the slice: x: 2, y: 2, z: 4, core: 2. Of those that a mesh axis runs over, the one named last changes fastest.
Arguments:
- covariates: bfloat16 [32768, 4096], P('row', 'col'), may hold values from -64 to 64
- labels: int32 [32768], P('row'), may hold values from 0 to 15
- weights: float32 [16, 4096], P(None, 'col'), may hold values from -0.0234375 to 0.0234375
- sample_index: int32 [16384], P('row'), may hold values from 0 to 32767, as said below
Outputs:
- gradient: float32 [16, 4096], P(None, 'col')
- newton_step: float32 [16, 4096], P(None, 'col')
The draws below stay inside these ranges and needn't reach their ends.
Inputs may be any that keep to these rules, and one draw needn't show every extreme that they name: The 4096 entries sample_index[b * 4096] to sample_index[(b + 1) * 4096 - 1] name users b * 8192 to (b + 1) * 8192 - 1; repeats may occur.
All inputs are finite; a program needn't handle non-finite values.
Results may differ from the reference program's by a relative error of at most 0.0039.
Values may be sent and summed in bfloat16 or wider, within the bound.
A program may use at most 64 MiB of HBM per device.

```python
import jax
import jax.numpy as jnp
from jax import lax

P_SIZE = 4096
K = 16
ITERS = 2
U_DEV = 8192
SUB_DEV = 4096
USERS = 32768
SUB = 16384
N_ROW = 4
N_COL = 8


def draw_sample_index(key, part):
    key = jax.random.fold_in(key, 7)
    within = jax.random.randint(key, (SUB,), 0, U_DEV)
    position = jnp.arange(SUB)
    within = jnp.where(position == 0, 0, within)
    within = jnp.where(position == SUB - 1, U_DEV - 1, within)
    return (position // SUB_DEV * U_DEV + within).astype(jnp.int32)


def draw_covariates(key, part):
    key = jax.random.fold_in(key, 11)
    keys = jax.random.split(key, 6)
    block_cols = P_SIZE // N_COL
    spread = 1.0
    noise = jnp.clip(jax.random.normal(keys[5], (N_ROW, U_DEV, N_COL, block_cols), jnp.float32), -4.0, 4.0)
    levels = jnp.exp(jax.random.uniform(keys[0], (N_ROW, N_COL), jnp.float32, -spread, spread))
    chance = jax.random.uniform(keys[1], (N_ROW, U_DEV), jnp.float32)
    forced = jax.random.randint(keys[2], (N_ROW, 1), 0, U_DEV)
    position = jnp.arange(U_DEV)[None, :]
    heavy = jnp.logical_or(chance < 1.0 / 256.0, position == forced)
    heavy_scale = jnp.exp(jax.random.uniform(keys[3], (N_ROW, U_DEV), jnp.float32, 1.386, 2.079))
    light_scale = jnp.exp(jax.random.uniform(keys[4], (N_ROW, U_DEV), jnp.float32, -2.303, -1.05))
    scale = jnp.where(heavy, heavy_scale, light_scale)
    values = noise * levels[:, None, :, None] * scale[:, :, None, None]
    values = jnp.clip(values, -64.0, 64.0)
    return values.reshape(USERS, P_SIZE).astype(jnp.bfloat16)


def place_ends(drawn, own_key, least, largest):
    spot = [jax.random.randint(jax.random.fold_in(own_key, axis), (), 0, length) for axis, length in enumerate(drawn.shape)]
    widest = drawn.shape.index(max(drawn.shape))
    next_to = spot[:widest] + [(spot[widest] + 1) % drawn.shape[widest]] + spot[widest + 1:]
    return drawn.at[tuple(spot)].set(least).at[tuple(next_to)].set(largest)


def level_of(key, shape, cuts, least, top_value):
    gain, own = 1.0, jax.random.fold_in(key, 6)
    for dim, blocks in cuts:
        steps = jnp.exp(jax.random.uniform(jax.random.fold_in(own, dim), (blocks,), jnp.float32, least / len(cuts), top_value / len(cuts)))
        gain = gain * jnp.repeat(steps, shape[dim] // blocks).reshape([-1 if axis == dim else 1 for axis in range(len(shape))])
    return gain


def gaussian(rng, extent, scale, reach, cuts=(), dtype=jnp.bfloat16):
    gain = level_of(rng, extent, cuts, -0.22, 0.18) if cuts else 1.0
    values = jax.random.normal(rng, extent, jnp.float32) * scale * gain
    return jnp.minimum(jnp.maximum(values, -reach), reach).astype(dtype)


def setup_inputs(seed: int = 0) -> dict:
    seeds = jax.random.split(jax.random.key(seed), 5)
    covariates = draw_covariates(jax.random.fold_in(seeds[4], 71), 0)
    labels = place_ends(jax.random.randint(seeds[1], (USERS,), 0, K), jax.random.fold_in(seeds[1], 1), 0, K - 1).astype(jnp.int32)
    weights = gaussian(seeds[2], (K, P_SIZE), (16 * P_SIZE) ** -0.5, 0.0234375, ((1, 8),), jnp.float32)
    sample_index = draw_sample_index(jax.random.fold_in(seeds[4], 71), 0)
    return dict(covariates=covariates, labels=labels, weights=weights, sample_index=sample_index)


RIDGE_WEIGHT = 0.004


def class_shares(logits):
    exponent = jnp.exp(logits)
    return exponent / jnp.sum(exponent, axis=0, keepdims=True)


def reference(covariates, labels, weights, sample_index):
    rounded_weights = weights.astype(jnp.bfloat16)
    logits = lax.dot_general(rounded_weights, covariates, (((1,), (1,)), ((), ())), preferred_element_type=jnp.float32)
    shares = class_shares(logits)
    classes = lax.broadcasted_iota(jnp.int32, shares.shape, 0)
    indicator = (labels[None, :] == classes).astype(jnp.float32)
    misfit = (shares - indicator).astype(jnp.bfloat16)
    gradient = jnp.dot(misfit, covariates, preferred_element_type=jnp.float32) / USERS + RIDGE_WEIGHT * weights
    sub_rows = jnp.take(covariates, sample_index.astype(jnp.int32), axis=0)
    sub_shares = jnp.take(shares, sample_index.astype(jnp.int32), axis=1)

    def hessian_apply(vector):
        rounded = vector.astype(jnp.bfloat16)
        response = lax.dot_general(rounded, sub_rows, (((1,), (1,)), ((), ())), preferred_element_type=jnp.float32)
        centred = response - jnp.sum(sub_shares * response, axis=0, keepdims=True)
        weighted = (sub_shares * centred).astype(jnp.bfloat16)
        return jnp.dot(weighted, sub_rows, preferred_element_type=jnp.float32) / SUB + RIDGE_WEIGHT * vector

    newton_step = jnp.zeros_like(weights)
    residual = -gradient
    direction = residual
    norm_now = jnp.sum(residual * residual)
    for iteration in range(ITERS):
        image = hessian_apply(direction)
        step_size = norm_now / jnp.sum(direction * image)
        newton_step = newton_step + step_size * direction
        residual = residual - step_size * image
        if iteration + 1 < ITERS:
            norm_new = jnp.sum(residual * residual)
            direction = residual + (norm_new / norm_now) * direction
            norm_now = norm_new
    return gradient, newton_step
```

```python
import functools

import jax
import jax.numpy as jnp
from jax import lax
from jax.experimental import pallas as pl
from jax.experimental.pallas import tpu as pltpu
from jax.sharding import PartitionSpec as P

ITERS = 2
RIDGE_WEIGHT = 0.004
LANES = 128
MESH = pl.DeviceIdType.MESH


def fold(value):
    value = value[:8] + value[8:]
    total = value[:, :LANES]
    for start in range(LANES, value.shape[1], LANES):
        total = total + value[:, start:start + LANES]
    return total


def kernel(
    n, rows, user_total, sub_total,
    cov_hbm, labels_ref, weights_ref, index_ref, gradient_ref, step_ref,
    cov, logit_send, logit_recv, resp_send, resp_recv, share_send, share_recv, row_buf, dot_send, dot_recv,
    cov_sem, rs_ssem, rs_rsem, ag_ssem, ag_rsem, row_ssem, row_rsem, dot_ssem, dot_rsem,
):
    me = lax.axis_index("col")
    my_row = lax.axis_index("row")
    chips = n // 2
    own = cov.shape[1]
    classes = weights_ref.shape[0]

    def target(j):
        return lax.rem(me // 2 + j // 2, chips) * 2 + lax.rem(lax.rem(me, 2) + lax.rem(j, 2), 2)

    def source(j):
        return lax.rem(me // 2 + chips - j // 2, chips) * 2 + lax.rem(lax.rem(me, 2) + 2 - lax.rem(j, 2), 2)

    def cov_copy(j):
        block = target(j)
        return pltpu.make_async_copy(cov_hbm.at[block], cov.at[block], cov_sem.at[j])

    def start_cov(i, carry):
        cov_copy(n - 1 - i).start()
        return carry

    lax.fori_loop(0, n, start_cov, 0)

    barrier = pltpu.get_barrier_semaphore()

    def greet_col(j, carry):
        pl.semaphore_signal(barrier, inc=1, device_id={"col": target(j)}, device_id_type=MESH)
        return carry

    def greet_row(t, carry):
        pl.semaphore_signal(
            barrier, inc=1, device_id={"row": lax.rem(my_row + t, rows)}, device_id_type=MESH
        )
        return carry

    lax.fori_loop(1, n, greet_col, 0)
    lax.fori_loop(1, rows, greet_row, 0)

    groups = own // LANES
    padded = max(16, groups)
    within = index_ref[...] - my_row * (n * own) - me * own
    lane = jnp.bitwise_and(within, LANES - 1)
    group = jnp.right_shift(within - lane, 7)
    group_hot = (lax.broadcasted_iota(jnp.int32, (padded, within.shape[1]), 0) == group)
    lane_hot = (lax.broadcasted_iota(jnp.int32, (LANES, within.shape[1]), 0) == lane)
    counts = lax.dot_general(
        group_hot.astype(jnp.float32).astype(jnp.bfloat16), lane_hot.astype(jnp.float32).astype(jnp.bfloat16),
        (((1,), (1,)), ((), ())), preferred_element_type=jnp.float32,
    )
    count = jnp.concatenate([counts[g:g + 1] for g in range(groups)], axis=1)

    pl.semaphore_wait(barrier, n - 1 + rows - 1)

    def rs_copy(phase, send, recv, j):
        return pltpu.make_async_remote_copy(
            src_ref=send.at[j], dst_ref=recv.at[j],
            send_sem=rs_ssem.at[phase, j], recv_sem=rs_rsem.at[phase, j],
            device_id={"col": target(j)}, device_id_type=MESH,
        )

    def project(vector, block):
        return lax.dot_general(
            vector, cov[block], (((1,), (1,)), ((), ())), preferred_element_type=jnp.float32
        )

    def reduce_users(phase, vector, send, recv):
        def one(i, carry):
            j = n - 1 - i
            if phase == 0:
                cov_copy(j).wait()
            send[j] = project(vector, target(j)).astype(send.dtype)
            rs_copy(phase, send, recv, j).start()
            return carry

        lax.fori_loop(0, n - 1, one, 0)
        if phase == 0:
            cov_copy(0).wait()

        def add(j, total):
            rs_copy(phase, send, recv, j).wait_recv()
            return total + recv[j].astype(jnp.float32)

        return lax.fori_loop(1, n, add, project(vector, me))

    def ag_copy(phase, j):
        return pltpu.make_async_remote_copy(
            src_ref=share_send.at[phase], dst_ref=share_recv.at[phase, j],
            send_sem=ag_ssem.at[phase, j], recv_sem=ag_rsem.at[phase, j],
            device_id={"col": target(j)}, device_id_type=MESH,
        )

    def row_copy(phase, t, slot):
        return pltpu.make_async_remote_copy(
            src_ref=row_buf.at[phase, my_row], dst_ref=row_buf.at[phase, slot],
            send_sem=row_ssem.at[phase, t], recv_sem=row_rsem.at[phase, t],
            device_id={"row": lax.rem(my_row + t, rows)}, device_id_type=MESH,
        )

    def back_project(phase, values):
        share_send[phase] = values

        def send(j, carry):
            ag_copy(phase, j).start()
            return carry

        lax.fori_loop(1, n, send, 0)

        def add(j, total):
            ag_copy(phase, j).wait_recv()
            return total + jnp.dot(
                share_recv[phase, j], cov[source(j)], preferred_element_type=jnp.float32
            )

        row_buf[phase, my_row] = lax.fori_loop(
            1, n, add, jnp.dot(values, cov[me], preferred_element_type=jnp.float32)
        )

        def send_row(t, carry):
            row_copy(phase, t, my_row).start()
            return carry

        def wait_row(t, carry):
            row_copy(phase, t, lax.rem(my_row + rows - t, rows)).wait_recv()
            return carry

        lax.fori_loop(1, rows, send_row, 0)
        lax.fori_loop(1, rows, wait_row, 0)
        total = row_buf[phase, 0]
        for r in range(1, rows):
            total = total + row_buf[phase, r]
        return total

    def dot_copy(phase, j):
        return pltpu.make_async_remote_copy(
            src_ref=dot_send.at[phase], dst_ref=dot_recv.at[phase, j],
            send_sem=dot_ssem.at[phase, j], recv_sem=dot_rsem.at[phase, j],
            device_id={"col": target(j)}, device_id_type=MESH,
        )

    def inner(phase, *pairs):
        for k, (first, second) in enumerate(pairs):
            dot_send[phase, k] = fold(first * second)

        def send(j, carry):
            dot_copy(phase, j).start()
            return carry

        def add(j, totals):
            dot_copy(phase, j).wait_recv()
            return tuple(total + dot_recv[phase, j, k] for k, total in enumerate(totals))

        lax.fori_loop(1, n, send, 0)
        totals = lax.fori_loop(1, n, add, tuple(dot_send[phase, k] for k in range(len(pairs))))
        return [jnp.sum(total, keepdims=True) for total in totals]

    weights = weights_ref[...]
    logits = reduce_users(0, weights.astype(jnp.bfloat16), logit_send, logit_recv)
    exponent = jnp.exp(logits)
    shares = exponent / jnp.sum(exponent, axis=0, keepdims=True)
    label = labels_ref[me]
    indicator = (label == lax.broadcasted_iota(jnp.int32, (classes, own), 0)).astype(jnp.float32)
    misfit = (shares - indicator).astype(jnp.bfloat16)
    gradient = back_project(0, misfit) / user_total + RIDGE_WEIGHT * weights
    gradient_ref[...] = gradient
    counted = count * shares

    residual = -gradient
    direction = residual
    newton_step = jnp.zeros_like(residual)
    norm_now = None
    for iteration in range(ITERS):
        response = reduce_users(
            iteration + 1, direction.astype(jnp.bfloat16), resp_send.at[iteration], resp_recv.at[iteration]
        )
        centred = response - jnp.sum(shares * response, axis=0, keepdims=True)
        weighted = (counted * centred).astype(jnp.bfloat16)
        image = back_project(iteration + 1, weighted) / sub_total + RIDGE_WEIGHT * direction
        if norm_now is None:
            curve, norm_now = inner(2 * iteration, (direction, image), (residual, residual))
        else:
            (curve,) = inner(2 * iteration, (direction, image))
        step_size = norm_now / curve
        newton_step = newton_step + step_size * direction
        residual = residual - step_size * image
        if iteration + 1 < ITERS:
            (norm_new,) = inner(2 * iteration + 1, (residual, residual))
            direction = residual + (norm_new / norm_now) * direction
            norm_now = norm_new
    step_ref[...] = newton_step

    def drain_col(j, carry):
        rs_copy(0, logit_send, logit_recv, j).wait_send()
        for phase in range(ITERS):
            rs_copy(phase + 1, resp_send.at[phase], resp_recv.at[phase], j).wait_send()
        for phase in range(ITERS + 1):
            ag_copy(phase, j).wait_send()
        for phase in range(2 * ITERS - 1):
            dot_copy(phase, j).wait_send()
        return carry

    def drain_row(t, carry):
        for phase in range(ITERS + 1):
            row_copy(phase, t, my_row).wait_send()
        return carry

    lax.fori_loop(1, n, drain_col, 0)
    lax.fori_loop(1, rows, drain_row, 0)


def body(covariates, labels, weights, sample_index):
    users, width = covariates.shape
    n, rows = lax.axis_size("col"), lax.axis_size("row")
    own = users // n
    classes = weights.shape[0]
    sub = sample_index.shape[0]
    dots = 2 * ITERS - 1
    dma = pltpu.SemaphoreType.DMA
    vmem = pl.BlockSpec(memory_space=pltpu.VMEM)
    return pl.pallas_call(
        functools.partial(kernel, n, rows, users * rows, sub * rows),
        out_shape=[jax.ShapeDtypeStruct((classes, width), jnp.float32)] * 2,
        in_specs=[pl.BlockSpec(memory_space=pl.ANY), vmem, vmem, vmem],
        out_specs=[vmem, vmem],
        scratch_shapes=[
            pltpu.VMEM((n, own, width), jnp.bfloat16),
            pltpu.VMEM((n, classes, own), jnp.float32),
            pltpu.VMEM((n, classes, own), jnp.float32),
            pltpu.VMEM((ITERS, n, classes, own), jnp.bfloat16),
            pltpu.VMEM((ITERS, n, classes, own), jnp.bfloat16),
            pltpu.VMEM((ITERS + 1, classes, own), jnp.bfloat16),
            pltpu.VMEM((ITERS + 1, n, classes, own), jnp.bfloat16),
            pltpu.VMEM((ITERS + 1, rows, classes, width), jnp.float32),
            pltpu.VMEM((dots, 2, 8, LANES), jnp.float32),
            pltpu.VMEM((dots, n, 2, 8, LANES), jnp.float32),
            dma((n,)),
            dma((ITERS + 1, n)), dma((ITERS + 1, n)),
            dma((ITERS + 1, n)), dma((ITERS + 1, n)),
            dma((ITERS + 1, rows)), dma((ITERS + 1, rows)),
            dma((dots, n)), dma((dots, n)),
        ],
        compiler_params=pltpu.CompilerParams(
            collective_id=0, has_side_effects=True, vmem_limit_bytes=40 * 1024 * 1024
        ),
        name="newton_step",
    )(
        covariates.reshape(n, own, width), labels.reshape(n, 1, own), weights, sample_index.reshape(1, sub)
    )


def solution(mesh):
    in_specs = (P("row", "col"), P("row"), P(None, "col"), P("row"))
    out_specs = (P(None, "col"), P(None, "col"))
    return jax.shard_map(body, mesh=mesh, in_specs=in_specs, out_specs=out_specs, check_vma=False)
```

```python
import functools

import jax
import jax.numpy as jnp
from jax import lax
from jax.experimental import pallas as pl
from jax.experimental.pallas import tpu as pltpu
from jax.sharding import PartitionSpec as P

ITERS = 2
RIDGE_WEIGHT = 0.004
LANES = 128
MESH = pl.DeviceIdType.MESH


def fold(value):
    value = value[:8] + value[8:]
    total = value[:, :LANES]
    for start in range(LANES, value.shape[1], LANES):
        total = total + value[:, start:start + LANES]
    return total


def kernel(
    n, rows, user_total, sub_total,
    cov_hbm, labels_hbm, weights_hbm, index_hbm, gradient_ref, step_ref,
    cov, labels_ref, weights_ref, index_ref, pair_send, pair_recv, logit_send, logit_recv, resp_send, resp_recv,
    share_send, share_recv, pass_recv, row_buf, dot_send, dot_recv,
    cov_sem, small_sem, pair_ssem, pair_rsem, rs_ssem, rs_rsem, ag_ssem, ag_rsem, pass_ssem, pass_rsem,
    row_ssem, row_rsem, dot_ssem, dot_rsem,
):
    me = lax.axis_index("col")
    my_row = lax.axis_index("row")
    chips = n // 2
    own = cov.shape[1]
    classes = weights_ref.shape[0]

    chip, core = me // 2, lax.rem(me, 2)
    sibling = chip * 2 + 1 - core

    def target(j):
        return lax.rem(me + j, n)

    def chip_after(s):
        return lax.rem(chip + s, chips)

    def chip_before(s):
        return lax.rem(chip + chips - s, chips)

    def theirs(i):
        return chip_after(chips - 1 - i) * 2 + 1 - core

    def mine(i):
        return chip_after(chips - 1 - i) * 2 + core

    def cov_copy(side, i):
        block = theirs(i) if side == 0 else mine(i)
        return pltpu.make_async_copy(cov_hbm.at[block], cov.at[block], cov_sem.at[side, i])

    small_copies = [
        pltpu.make_async_copy(weights_hbm, weights_ref, small_sem.at[0]),
        pltpu.make_async_copy(index_hbm, index_ref, small_sem.at[1]),
        pltpu.make_async_copy(labels_hbm.at[me], labels_ref, small_sem.at[2]),
    ]
    for copy in small_copies:
        copy.start()

    def start_cov(i, carry):
        cov_copy(0, i).start()
        cov_copy(1, i).start()
        return carry

    lax.fori_loop(0, chips, start_cov, 0)

    barrier = pltpu.get_barrier_semaphore()

    def greet_col(j, carry):
        pl.semaphore_signal(barrier, inc=1, device_id={"col": target(j)}, device_id_type=MESH)
        return carry

    def greet_row(t, carry):
        pl.semaphore_signal(
            barrier, inc=1, device_id={"row": lax.rem(my_row + t, rows)}, device_id_type=MESH
        )
        return carry

    lax.fori_loop(1, n, greet_col, 0)
    lax.fori_loop(1, rows, greet_row, 0)

    for copy in small_copies:
        copy.wait()

    groups = own // LANES
    padded = max(16, groups)
    within = index_ref[...] - my_row * (n * own) - me * own
    lane = jnp.bitwise_and(within, LANES - 1)
    group = jnp.right_shift(within - lane, 7)
    group_hot = (lax.broadcasted_iota(jnp.int32, (padded, within.shape[1]), 0) == group)
    lane_hot = (lax.broadcasted_iota(jnp.int32, (LANES, within.shape[1]), 0) == lane)
    counts = lax.dot_general(
        group_hot.astype(jnp.float32).astype(jnp.bfloat16), lane_hot.astype(jnp.float32).astype(jnp.bfloat16),
        (((1,), (1,)), ((), ())), preferred_element_type=jnp.float32,
    )
    count = jnp.concatenate([counts[g:g + 1] for g in range(groups)], axis=1)

    pl.semaphore_wait(barrier, n - 1 + rows - 1)

    def pair_copy(phase, i):
        return pltpu.make_async_remote_copy(
            src_ref=pair_send.at[phase, i], dst_ref=pair_recv.at[phase, i],
            send_sem=pair_ssem.at[phase, i], recv_sem=pair_rsem.at[phase, i],
            device_id={"col": sibling}, device_id_type=MESH,
        )

    def rs_copy(phase, send, recv, i):
        return pltpu.make_async_remote_copy(
            src_ref=send.at[i], dst_ref=recv.at[i],
            send_sem=rs_ssem.at[phase, i], recv_sem=rs_rsem.at[phase, i],
            device_id={"col": mine(i)}, device_id_type=MESH,
        )

    def project(vector, block):
        return lax.dot_general(
            vector, cov[block], (((1,), (1,)), ((), ())), preferred_element_type=jnp.float32
        )

    def reduce_users(phase, vector, send, recv):
        def for_sibling(i):
            if phase == 0:
                cov_copy(0, i).wait()
            pair_send[phase, i] = project(vector, theirs(i))
            pair_copy(phase, i).start()

        def for_own(i):
            if phase == 0:
                cov_copy(1, i).wait()
            part = project(vector, mine(i))
            pair_copy(phase, i).wait_recv()
            return part + pair_recv[phase, i]

        def send_own(i):
            send[i] = for_own(i).astype(send.dtype)
            rs_copy(phase, send, recv, i).start()

        def both(i, carry):
            send_own(i)
            for_sibling(i + 2)
            return carry

        for_sibling(0)
        for_sibling(1)
        lax.fori_loop(0, chips - 2, both, 0)
        send_own(chips - 2)

        def add(i, total):
            rs_copy(phase, send, recv, i).wait_recv()
            return total + recv[i].astype(jnp.float32)

        return lax.fori_loop(0, chips - 1, add, for_own(chips - 1))

    def ag_copy(phase, s):
        peer = sibling if s is None else chip_after(s) * 2 + core
        slot = 0 if s is None else s
        return pltpu.make_async_remote_copy(
            src_ref=share_send.at[phase], dst_ref=share_recv.at[phase, slot],
            send_sem=ag_ssem.at[phase, slot], recv_sem=ag_rsem.at[phase, slot],
            device_id={"col": peer}, device_id_type=MESH,
        )

    def forward(phase, s):
        return pltpu.make_async_remote_copy(
            src_ref=share_recv.at[phase, s], dst_ref=pass_recv.at[phase, s],
            send_sem=pass_ssem.at[phase, s], recv_sem=pass_rsem.at[phase, s],
            device_id={"col": sibling}, device_id_type=MESH,
        )

    def row_copy(phase, t, slot):
        return pltpu.make_async_remote_copy(
            src_ref=row_buf.at[phase, my_row], dst_ref=row_buf.at[phase, slot],
            send_sem=row_ssem.at[phase, t], recv_sem=row_rsem.at[phase, t],
            device_id={"row": lax.rem(my_row + t, rows)}, device_id_type=MESH,
        )

    def back_project(phase, values):
        share_send[phase] = values

        ag_copy(phase, None).start()

        def send(s, carry):
            ag_copy(phase, s).start()
            return carry

        lax.fori_loop(1, chips, send, 0)

        def term(block_values, block):
            return jnp.dot(block_values, cov[block], preferred_element_type=jnp.float32)

        def direct(s):
            ag_copy(phase, s).wait_recv()
            forward(phase, s).start()
            return term(share_recv[phase, s], chip_before(s) * 2 + core)

        def passed(s):
            forward(phase, s).wait_recv()
            return term(pass_recv[phase, s], chip_before(s) * 2 + 1 - core)

        def both(s, total):
            return total + direct(s + 1) + passed(s)

        total = term(values, me)
        ag_copy(phase, None).wait_recv()
        total = total + term(share_recv[phase, 0], sibling) + direct(1)
        total = lax.fori_loop(1, chips - 1, both, total)
        row_buf[phase, my_row] = total + passed(chips - 1)

        def send_row(t, carry):
            row_copy(phase, t, my_row).start()
            return carry

        def wait_row(t, carry):
            row_copy(phase, t, lax.rem(my_row + rows - t, rows)).wait_recv()
            return carry

        lax.fori_loop(1, rows, send_row, 0)
        lax.fori_loop(1, rows, wait_row, 0)
        total = row_buf[phase, 0]
        for r in range(1, rows):
            total = total + row_buf[phase, r]
        return total

    def dot_copy(phase, j):
        return pltpu.make_async_remote_copy(
            src_ref=dot_send.at[phase], dst_ref=dot_recv.at[phase, j],
            send_sem=dot_ssem.at[phase, j], recv_sem=dot_rsem.at[phase, j],
            device_id={"col": target(j)}, device_id_type=MESH,
        )

    def inner(phase, *pairs):
        for k, (first, second) in enumerate(pairs):
            dot_send[phase, k] = fold(first * second)

        def send(j, carry):
            dot_copy(phase, j).start()
            return carry

        def add(j, totals):
            dot_copy(phase, j).wait_recv()
            return tuple(total + dot_recv[phase, j, k] for k, total in enumerate(totals))

        lax.fori_loop(1, n, send, 0)
        totals = lax.fori_loop(1, n, add, tuple(dot_send[phase, k] for k in range(len(pairs))))
        return [jnp.sum(total, keepdims=True) for total in totals]

    weights = weights_ref[...]
    logits = reduce_users(0, weights.astype(jnp.bfloat16), logit_send, logit_recv)
    exponent = jnp.exp(logits)
    shares = exponent / jnp.sum(exponent, axis=0, keepdims=True)
    label = labels_ref[...]
    indicator = (label == lax.broadcasted_iota(jnp.int32, (classes, own), 0)).astype(jnp.float32)
    misfit = (shares - indicator).astype(jnp.bfloat16)
    gradient = back_project(0, misfit) / user_total + RIDGE_WEIGHT * weights
    gradient_ref[...] = gradient
    counted = count * shares

    residual = -gradient
    direction = residual
    newton_step = jnp.zeros_like(residual)
    norm_now = None
    for iteration in range(ITERS):
        response = reduce_users(
            iteration + 1, direction.astype(jnp.bfloat16), resp_send.at[iteration], resp_recv.at[iteration]
        )
        centred = response - jnp.sum(shares * response, axis=0, keepdims=True)
        weighted = (counted * centred).astype(jnp.bfloat16)
        image = back_project(iteration + 1, weighted) / sub_total + RIDGE_WEIGHT * direction
        if norm_now is None:
            curve, norm_now = inner(2 * iteration, (direction, image), (residual, residual))
        else:
            (curve,) = inner(2 * iteration, (direction, image))
        step_size = norm_now / curve
        newton_step = newton_step + step_size * direction
        residual = residual - step_size * image
        if iteration + 1 < ITERS:
            (norm_new,) = inner(2 * iteration + 1, (residual, residual))
            direction = residual + (norm_new / norm_now) * direction
            norm_now = norm_new
    step_ref[...] = newton_step

    def drain_pair(i, carry):
        for phase in range(ITERS + 1):
            pair_copy(phase, i).wait_send()
        return carry

    def drain_chip(s, carry):
        rs_copy(0, logit_send, logit_recv, s - 1).wait_send()
        for phase in range(ITERS):
            rs_copy(phase + 1, resp_send.at[phase], resp_recv.at[phase], s - 1).wait_send()
        for phase in range(ITERS + 1):
            ag_copy(phase, s).wait_send()
            forward(phase, s).wait_send()
        return carry

    def drain_col(j, carry):
        for phase in range(2 * ITERS - 1):
            dot_copy(phase, j).wait_send()
        return carry

    def drain_row(t, carry):
        for phase in range(ITERS + 1):
            row_copy(phase, t, my_row).wait_send()
        return carry

    for phase in range(ITERS + 1):
        ag_copy(phase, None).wait_send()
    lax.fori_loop(0, chips, drain_pair, 0)
    lax.fori_loop(1, chips, drain_chip, 0)
    lax.fori_loop(1, n, drain_col, 0)
    lax.fori_loop(1, rows, drain_row, 0)


def body(covariates, labels, weights, sample_index):
    users, width = covariates.shape
    n, rows = lax.axis_size("col"), lax.axis_size("row")
    own, chips = users // n, n // 2
    classes = weights.shape[0]
    sub = sample_index.shape[0]
    dots = 2 * ITERS - 1
    dma = pltpu.SemaphoreType.DMA
    vmem = pl.BlockSpec(memory_space=pltpu.VMEM)
    return pl.pallas_call(
        functools.partial(kernel, n, rows, users * rows, sub * rows),
        out_shape=[jax.ShapeDtypeStruct((classes, width), jnp.float32)] * 2,
        in_specs=[pl.BlockSpec(memory_space=pltpu.HBM)] * 4,
        out_specs=[vmem, vmem],
        scratch_shapes=[
            pltpu.VMEM((n, own, width), jnp.bfloat16),
            pltpu.VMEM((1, own), jnp.int32),
            pltpu.VMEM((classes, width), jnp.float32),
            pltpu.VMEM((1, sub), jnp.int32),
            pltpu.VMEM((ITERS + 1, chips, classes, own), jnp.float32),
            pltpu.VMEM((ITERS + 1, chips, classes, own), jnp.float32),
            pltpu.VMEM((chips, classes, own), jnp.float32),
            pltpu.VMEM((chips, classes, own), jnp.float32),
            pltpu.VMEM((ITERS, chips, classes, own), jnp.bfloat16),
            pltpu.VMEM((ITERS, chips, classes, own), jnp.bfloat16),
            pltpu.VMEM((ITERS + 1, classes, own), jnp.bfloat16),
            pltpu.VMEM((ITERS + 1, chips, classes, own), jnp.bfloat16),
            pltpu.VMEM((ITERS + 1, chips, classes, own), jnp.bfloat16),
            pltpu.VMEM((ITERS + 1, rows, classes, width), jnp.float32),
            pltpu.VMEM((dots, 2, 8, LANES), jnp.float32),
            pltpu.VMEM((dots, n, 2, 8, LANES), jnp.float32),
            dma((2, chips)), dma((3,)),
            dma((ITERS + 1, chips)), dma((ITERS + 1, chips)),
            dma((ITERS + 1, chips)), dma((ITERS + 1, chips)),
            dma((ITERS + 1, chips)), dma((ITERS + 1, chips)),
            dma((ITERS + 1, chips)), dma((ITERS + 1, chips)),
            dma((ITERS + 1, rows)), dma((ITERS + 1, rows)),
            dma((dots, n)), dma((dots, n)),
        ],
        compiler_params=pltpu.CompilerParams(
            collective_id=0, has_side_effects=True, vmem_limit_bytes=40 * 1024 * 1024
        ),
        name="newton_step",
    )(
        covariates.reshape(n, own, width), labels.reshape(n, 1, own), weights, sample_index.reshape(1, sub)
    )


def solution(mesh):
    in_specs = (P("row", "col"), P("row"), P(None, "col"), P("row"))
    out_specs = (P(None, "col"), P(None, "col"))
    return jax.shard_map(body, mesh=mesh, in_specs=in_specs, out_specs=out_specs, check_vma=False)
```

```python
import functools

import jax
import jax.numpy as jnp
from jax import lax
from jax.experimental import pallas as pl
from jax.experimental.pallas import tpu as pltpu
from jax.sharding import PartitionSpec as P

ITERS = 2
RIDGE_WEIGHT = 0.004
LANES = 128
MESH = pl.DeviceIdType.MESH


def fold(value):
    value = value[:8] + value[8:]
    total = value[:, :LANES]
    for start in range(LANES, value.shape[1], LANES):
        total = total + value[:, start:start + LANES]
    return total


def kernel(
    n, rows, user_total, sub_total,
    cov_hbm, labels_hbm, weights_hbm, index_hbm, out_ref,
    cov, labels_ref, weights_ref, index_ref, pair_send, pair_recv, logit_send, logit_recv, resp_send, resp_recv,
    share_send, share_recv, pass_recv, row_buf, curve_buf, dot_send, dot_recv,
    cov_sem, small_sem, pair_ssem, pair_rsem, rs_ssem, rs_rsem, ag_ssem, ag_rsem, pass_ssem, pass_rsem,
    row_ssem, row_rsem, curve_ssem, curve_rsem, dot_ssem, dot_rsem,
):
    me = lax.axis_index("col")
    my_row = lax.axis_index("row")
    chips = n // 2
    own = cov.shape[1]
    classes = weights_ref.shape[0]

    chip, core = me // 2, lax.rem(me, 2)
    sibling = chip * 2 + 1 - core

    def target(j):
        return lax.rem(me + j, n)

    def chip_after(s):
        return lax.rem(chip + s, chips)

    def chip_before(s):
        return lax.rem(chip + chips - s, chips)

    def theirs(i):
        return chip_after(chips - 1 - i) * 2 + 1 - core

    def mine(i):
        return chip_after(chips - 1 - i) * 2 + core

    def cov_copy(side, i):
        block = theirs(i) if side == 0 else mine(i)
        return pltpu.make_async_copy(cov_hbm.at[block], cov.at[block], cov_sem.at[side, i])

    small_copies = [
        pltpu.make_async_copy(weights_hbm, weights_ref, small_sem.at[0]),
        pltpu.make_async_copy(index_hbm, index_ref, small_sem.at[1]),
        pltpu.make_async_copy(labels_hbm.at[me], labels_ref, small_sem.at[2]),
    ]
    for copy in small_copies:
        copy.start()

    def start_cov(i, carry):
        cov_copy(0, i).start()
        cov_copy(1, i).start()
        return carry

    lax.fori_loop(0, chips, start_cov, 0)

    barrier = pltpu.get_barrier_semaphore()

    def greet_col(j, carry):
        pl.semaphore_signal(barrier, inc=1, device_id={"col": target(j)}, device_id_type=MESH)
        return carry

    def greet_row(t, carry):
        pl.semaphore_signal(
            barrier, inc=1, device_id={"row": lax.rem(my_row + t, rows)}, device_id_type=MESH
        )
        return carry

    lax.fori_loop(1, n, greet_col, 0)
    lax.fori_loop(1, rows, greet_row, 0)

    for copy in small_copies:
        copy.wait()

    groups = own // LANES
    padded = max(16, groups)
    within = index_ref[...] - my_row * (n * own) - me * own
    lane = jnp.bitwise_and(within, LANES - 1)
    group = jnp.right_shift(within - lane, 7)
    group_hot = (lax.broadcasted_iota(jnp.int32, (padded, within.shape[1]), 0) == group)
    lane_hot = (lax.broadcasted_iota(jnp.int32, (LANES, within.shape[1]), 0) == lane)
    counts = lax.dot_general(
        group_hot.astype(jnp.float32).astype(jnp.bfloat16), lane_hot.astype(jnp.float32).astype(jnp.bfloat16),
        (((1,), (1,)), ((), ())), preferred_element_type=jnp.float32,
    )
    count = jnp.concatenate([counts[g:g + 1] for g in range(groups)], axis=1)

    pl.semaphore_wait(barrier, n - 1 + rows - 1)

    def pair_copy(phase, i):
        return pltpu.make_async_remote_copy(
            src_ref=pair_send.at[phase, i], dst_ref=pair_recv.at[phase, i],
            send_sem=pair_ssem.at[phase, i], recv_sem=pair_rsem.at[phase, i],
            device_id={"col": sibling}, device_id_type=MESH,
        )

    def rs_copy(phase, send, recv, i):
        return pltpu.make_async_remote_copy(
            src_ref=send.at[i], dst_ref=recv.at[i],
            send_sem=rs_ssem.at[phase, i], recv_sem=rs_rsem.at[phase, i],
            device_id={"col": mine(i)}, device_id_type=MESH,
        )

    def project(vector, block):
        return lax.dot_general(
            vector, cov[block], (((1,), (1,)), ((), ())), preferred_element_type=jnp.float32
        )

    def reduce_users(phase, vector, send, recv):
        def for_sibling(i):
            if phase == 0:
                cov_copy(0, i).wait()
            pair_send[phase, i] = project(vector, theirs(i))
            pair_copy(phase, i).start()

        def for_own(i):
            if phase == 0:
                cov_copy(1, i).wait()
            part = project(vector, mine(i))
            pair_copy(phase, i).wait_recv()
            return part + pair_recv[phase, i]

        def send_own(i):
            send[i] = for_own(i).astype(send.dtype)
            rs_copy(phase, send, recv, i).start()

        def both(i, carry):
            send_own(i)
            for_sibling(i + 2)
            return carry

        for_sibling(0)
        for_sibling(1)
        lax.fori_loop(0, chips - 2, both, 0)
        send_own(chips - 2)

        def add(i, total):
            rs_copy(phase, send, recv, i).wait_recv()
            return total + recv[i].astype(jnp.float32)

        return lax.fori_loop(0, chips - 1, add, for_own(chips - 1))

    def ag_copy(phase, s):
        peer = sibling if s is None else chip_after(s) * 2 + core
        slot = 0 if s is None else s
        return pltpu.make_async_remote_copy(
            src_ref=share_send.at[phase], dst_ref=share_recv.at[phase, slot],
            send_sem=ag_ssem.at[phase, slot], recv_sem=ag_rsem.at[phase, slot],
            device_id={"col": peer}, device_id_type=MESH,
        )

    def forward(phase, s):
        return pltpu.make_async_remote_copy(
            src_ref=share_recv.at[phase, s], dst_ref=pass_recv.at[phase, s],
            send_sem=pass_ssem.at[phase, s], recv_sem=pass_rsem.at[phase, s],
            device_id={"col": sibling}, device_id_type=MESH,
        )

    def row_copy(phase, t, slot):
        return pltpu.make_async_remote_copy(
            src_ref=row_buf.at[phase, my_row], dst_ref=row_buf.at[phase, slot],
            send_sem=row_ssem.at[phase, t], recv_sem=row_rsem.at[phase, t],
            device_id={"row": lax.rem(my_row + t, rows)}, device_id_type=MESH,
        )

    def back_project(phase, values, meanwhile=None):
        share_send[phase] = values

        ag_copy(phase, None).start()

        def send(s, carry):
            ag_copy(phase, s).start()
            return carry

        lax.fori_loop(1, chips, send, 0)

        def term(block_values, block):
            return jnp.dot(block_values, cov[block], preferred_element_type=jnp.float32)

        def direct(s):
            ag_copy(phase, s).wait_recv()
            forward(phase, s).start()
            return term(share_recv[phase, s], chip_before(s) * 2 + core)

        def passed(s):
            forward(phase, s).wait_recv()
            return term(pass_recv[phase, s], chip_before(s) * 2 + 1 - core)

        def both(s, total):
            return total + direct(s + 1) + passed(s)

        total = term(values, me)
        ag_copy(phase, None).wait_recv()
        total = total + term(share_recv[phase, 0], sibling) + direct(1)
        total = lax.fori_loop(1, chips - 1, both, total)
        if meanwhile is not None:
            meanwhile()
        row_buf[phase, my_row] = total + passed(chips - 1)

        def send_row(t, carry):
            row_copy(phase, t, my_row).start()
            return carry

        def wait_row(t, carry):
            row_copy(phase, t, lax.rem(my_row + rows - t, rows)).wait_recv()
            return carry

        lax.fori_loop(1, rows, send_row, 0)
        lax.fori_loop(1, rows, wait_row, 0)
        total = row_buf[phase, 0]
        for r in range(1, rows):
            total = total + row_buf[phase, r]
        return total

    def dot_copy(phase, j):
        return pltpu.make_async_remote_copy(
            src_ref=dot_send.at[phase], dst_ref=dot_recv.at[phase, j],
            send_sem=dot_ssem.at[phase, j], recv_sem=dot_rsem.at[phase, j],
            device_id={"col": target(j)}, device_id_type=MESH,
        )

    def send_dots(phase, *tiles):
        for k, tile in enumerate(tiles):
            dot_send[phase, k] = tile

        def send(j, carry):
            dot_copy(phase, j).start()
            return carry

        lax.fori_loop(1, n, send, 0)

    def take_dots(phase, tiles):
        def add(j, totals):
            dot_copy(phase, j).wait_recv()
            return tuple(total + dot_recv[phase, j, k] for k, total in enumerate(totals))

        totals = lax.fori_loop(1, n, add, tuple(dot_send[phase, k] for k in range(tiles)))
        return [jnp.sum(total, keepdims=True) for total in totals]

    def curve_copy(phase, t, slot):
        return pltpu.make_async_remote_copy(
            src_ref=curve_buf.at[phase, my_row], dst_ref=curve_buf.at[phase, slot],
            send_sem=curve_ssem.at[phase, t], recv_sem=curve_rsem.at[phase, t],
            device_id={"row": lax.rem(my_row + t, rows)}, device_id_type=MESH,
        )

    def send_curve(phase, tile):
        curve_buf[phase, my_row] = tile

        def send(t, carry):
            curve_copy(phase, t, my_row).start()
            return carry

        lax.fori_loop(1, rows, send, 0)

    def take_curve(phase):
        def wait(t, carry):
            curve_copy(phase, t, lax.rem(my_row + rows - t, rows)).wait_recv()
            return carry

        lax.fori_loop(1, rows, wait, 0)
        total = curve_buf[phase, 0]
        for r in range(1, rows):
            total = total + curve_buf[phase, r]
        return total

    weights = weights_ref[...]
    logits = reduce_users(0, weights.astype(jnp.bfloat16), logit_send, logit_recv)
    exponent = jnp.exp(logits)
    shares = exponent / jnp.sum(exponent, axis=0, keepdims=True)
    label = labels_ref[...]
    indicator = (label == lax.broadcasted_iota(jnp.int32, (classes, own), 0)).astype(jnp.float32)
    misfit = (shares - indicator).astype(jnp.bfloat16)
    gradient = back_project(0, misfit) / user_total + RIDGE_WEIGHT * weights
    out_ref[0] = gradient
    counted = count * shares

    residual = -gradient
    direction = residual
    newton_step = jnp.zeros_like(residual)
    norm_now = step_size = image = residual_response = direction_response = None
    for iteration in range(ITERS):
        last = iteration + 1 == ITERS
        vector = direction if iteration == 0 else image
        response = reduce_users(
            iteration + 1, vector.astype(jnp.bfloat16), resp_send.at[iteration], resp_recv.at[iteration]
        )
        if iteration == 0:
            residual_response = direction_response = response
        else:
            (norm_new,) = take_dots(2 * iteration - 1, 1)
            ratio = norm_new / norm_now
            direction = residual + ratio * direction
            norm_now = norm_new
            residual_response = residual_response - step_size * response
            direction_response = residual_response + ratio * direction_response
        centred = direction_response - jnp.sum(shares * direction_response, axis=0, keepdims=True)
        weighted = (counted * centred).astype(jnp.bfloat16)
        send_curve(iteration, fold(weighted.astype(jnp.float32) * direction_response))
        square = fold(direction * direction)

        def pass_curve():
            tiles = [take_curve(iteration) / sub_total + RIDGE_WEIGHT * square]
            send_dots(2 * iteration, *(tiles + [square] if iteration == 0 else tiles))

        if last:
            pass_curve()
        else:
            image = back_project(iteration + 1, weighted, pass_curve) / sub_total + RIDGE_WEIGHT * direction
        if iteration == 0:
            curve, norm_now = take_dots(0, 2)
        else:
            (curve,) = take_dots(2 * iteration, 1)
        step_size = norm_now / curve
        newton_step = newton_step + step_size * direction
        if not last:
            residual = residual - step_size * image
            send_dots(2 * iteration + 1, fold(residual * residual))
    out_ref[1] = newton_step

    def drain_pair(i, carry):
        for phase in range(ITERS + 1):
            pair_copy(phase, i).wait_send()
        return carry

    def drain_chip(s, carry):
        rs_copy(0, logit_send, logit_recv, s - 1).wait_send()
        for phase in range(ITERS):
            rs_copy(phase + 1, resp_send.at[phase], resp_recv.at[phase], s - 1).wait_send()
        for phase in range(ITERS):
            ag_copy(phase, s).wait_send()
            forward(phase, s).wait_send()
        return carry

    def drain_col(j, carry):
        for phase in range(2 * ITERS - 1):
            dot_copy(phase, j).wait_send()
        return carry

    def drain_row(t, carry):
        for phase in range(ITERS):
            row_copy(phase, t, my_row).wait_send()
            curve_copy(phase, t, my_row).wait_send()
        return carry

    for phase in range(ITERS):
        ag_copy(phase, None).wait_send()
    lax.fori_loop(0, chips, drain_pair, 0)
    lax.fori_loop(1, chips, drain_chip, 0)
    lax.fori_loop(1, n, drain_col, 0)
    lax.fori_loop(1, rows, drain_row, 0)


def body(covariates, labels, weights, sample_index):
    users, width = covariates.shape
    n, rows = lax.axis_size("col"), lax.axis_size("row")
    own, chips = users // n, n // 2
    classes = weights.shape[0]
    sub = sample_index.shape[0]
    dots = 2 * ITERS - 1
    dma = pltpu.SemaphoreType.DMA
    out = pl.pallas_call(
        functools.partial(kernel, n, rows, users * rows, sub * rows),
        out_shape=jax.ShapeDtypeStruct((2, classes, width), jnp.float32),
        in_specs=[pl.BlockSpec(memory_space=pltpu.HBM)] * 4,
        out_specs=pl.BlockSpec(memory_space=pltpu.VMEM),
        scratch_shapes=[
            pltpu.VMEM((n, own, width), jnp.bfloat16),
            pltpu.VMEM((1, own), jnp.int32),
            pltpu.VMEM((classes, width), jnp.float32),
            pltpu.VMEM((1, sub), jnp.int32),
            pltpu.VMEM((ITERS + 1, chips, classes, own), jnp.float32),
            pltpu.VMEM((ITERS + 1, chips, classes, own), jnp.float32),
            pltpu.VMEM((chips, classes, own), jnp.float32),
            pltpu.VMEM((chips, classes, own), jnp.float32),
            pltpu.VMEM((ITERS, chips, classes, own), jnp.bfloat16),
            pltpu.VMEM((ITERS, chips, classes, own), jnp.bfloat16),
            pltpu.VMEM((ITERS, classes, own), jnp.bfloat16),
            pltpu.VMEM((ITERS, chips, classes, own), jnp.bfloat16),
            pltpu.VMEM((ITERS, chips, classes, own), jnp.bfloat16),
            pltpu.VMEM((ITERS, rows, classes, width), jnp.float32),
            pltpu.VMEM((ITERS, rows, 8, LANES), jnp.float32),
            pltpu.VMEM((dots, 2, 8, LANES), jnp.float32),
            pltpu.VMEM((dots, n, 2, 8, LANES), jnp.float32),
            dma((2, chips)), dma((3,)),
            dma((ITERS + 1, chips)), dma((ITERS + 1, chips)),
            dma((ITERS + 1, chips)), dma((ITERS + 1, chips)),
            dma((ITERS, chips)), dma((ITERS, chips)),
            dma((ITERS, chips)), dma((ITERS, chips)),
            dma((ITERS, rows)), dma((ITERS, rows)),
            dma((ITERS, rows)), dma((ITERS, rows)),
            dma((dots, n)), dma((dots, n)),
        ],
        compiler_params=pltpu.CompilerParams(
            collective_id=0, has_side_effects=True, vmem_limit_bytes=60 * 1024 * 1024
        ),
        name="newton_step",
    )(
        covariates.reshape(n, own, width), labels.reshape(n, 1, own), weights, sample_index.reshape(1, sub)
    )
    return out[0], out[1]


def solution(mesh):
    in_specs = (P("row", "col"), P("row"), P(None, "col"), P("row"))
    out_specs = (P(None, "col"), P(None, "col"))
    return jax.shard_map(body, mesh=mesh, in_specs=in_specs, out_specs=out_specs, check_vma=False)
```

```python
import functools

import jax
import jax.numpy as jnp
from jax import lax
from jax.experimental import pallas as pl
from jax.experimental.pallas import tpu as pltpu
from jax.sharding import PartitionSpec as P

ITERS = 2
RIDGE_WEIGHT = 0.004
LANES = 128
MESH = pl.DeviceIdType.MESH


def fold(value):
    value = value[:8] + value[8:]
    total = value[:, :LANES]
    for start in range(LANES, value.shape[1], LANES):
        total = total + value[:, start:start + LANES]
    return total


def kernel(
    n, rows, user_total, sub_total,
    cov_hbm, labels_hbm, weights_hbm, index_hbm, gradient_ref, step_ref,
    cov, labels_ref, weights_ref, index_ref, pair_send, pair_recv, logit_send, logit_recv, resp_send, resp_recv,
    share_send, share_recv, pass_recv, row_buf, curve_buf, dot_send, dot_recv,
    cov_sem, small_sem, pair_ssem, pair_rsem, rs_ssem, rs_rsem, ag_ssem, ag_rsem, pass_ssem, pass_rsem,
    row_ssem, row_rsem, curve_ssem, curve_rsem, dot_ssem, dot_rsem,
):
    me = lax.axis_index("col")
    my_row = lax.axis_index("row")
    chips = n // 2
    own = cov.shape[1]
    classes = weights_ref.shape[0]

    chip, core = me // 2, lax.rem(me, 2)
    sibling = chip * 2 + 1 - core

    def target(j):
        return lax.rem(me + j, n)

    def chip_after(s):
        return lax.rem(chip + s, chips)

    def chip_before(s):
        return lax.rem(chip + chips - s, chips)

    def theirs(i):
        return chip_after(chips - 1 - i) * 2 + 1 - core

    def mine(i):
        return chip_after(chips - 1 - i) * 2 + core

    def cov_copy(side, i):
        block = theirs(i) if side == 0 else mine(i)
        return pltpu.make_async_copy(cov_hbm.at[block], cov.at[block], cov_sem.at[side, i])

    small_copies = [
        pltpu.make_async_copy(weights_hbm, weights_ref, small_sem.at[0]),
        pltpu.make_async_copy(index_hbm, index_ref, small_sem.at[1]),
        pltpu.make_async_copy(labels_hbm.at[me], labels_ref, small_sem.at[2]),
    ]
    for copy in small_copies:
        copy.start()

    def start_cov(i, carry):
        cov_copy(0, i).start()
        cov_copy(1, i).start()
        return carry

    lax.fori_loop(0, chips, start_cov, 0)

    barrier = pltpu.get_barrier_semaphore()

    def greet_col(j, carry):
        pl.semaphore_signal(barrier, inc=1, device_id={"col": target(j)}, device_id_type=MESH)
        return carry

    def greet_row(t, carry):
        pl.semaphore_signal(
            barrier, inc=1, device_id={"row": lax.rem(my_row + t, rows)}, device_id_type=MESH
        )
        return carry

    lax.fori_loop(1, n, greet_col, 0)
    lax.fori_loop(1, rows, greet_row, 0)

    for copy in small_copies:
        copy.wait()

    groups = own // LANES
    padded = max(16, groups)
    within = index_ref[...] - my_row * (n * own) - me * own
    lane = jnp.bitwise_and(within, LANES - 1)
    group = jnp.right_shift(within - lane, 7)
    group_hot = (lax.broadcasted_iota(jnp.int32, (padded, within.shape[1]), 0) == group)
    lane_hot = (lax.broadcasted_iota(jnp.int32, (LANES, within.shape[1]), 0) == lane)
    counts = lax.dot_general(
        group_hot.astype(jnp.float32).astype(jnp.bfloat16), lane_hot.astype(jnp.float32).astype(jnp.bfloat16),
        (((1,), (1,)), ((), ())), preferred_element_type=jnp.float32,
    )
    count = jnp.concatenate([counts[g:g + 1] for g in range(groups)], axis=1)

    pl.semaphore_wait(barrier, n - 1 + rows - 1)

    def pair_copy(phase, i):
        return pltpu.make_async_remote_copy(
            src_ref=pair_send.at[phase, i], dst_ref=pair_recv.at[phase, i],
            send_sem=pair_ssem.at[phase, i], recv_sem=pair_rsem.at[phase, i],
            device_id={"col": sibling}, device_id_type=MESH,
        )

    def rs_copy(phase, send, recv, i):
        return pltpu.make_async_remote_copy(
            src_ref=send.at[i], dst_ref=recv.at[i],
            send_sem=rs_ssem.at[phase, i], recv_sem=rs_rsem.at[phase, i],
            device_id={"col": mine(i)}, device_id_type=MESH,
        )

    def project(vector, block):
        return jnp.dot(cov[block], vector, preferred_element_type=jnp.float32).T

    def reduce_users(phase, vector, send, recv):
        vector = vector.T.astype(jnp.bfloat16)

        def for_sibling(i):
            if phase == 0:
                cov_copy(0, i).wait()
            pair_send[phase, i] = project(vector, theirs(i))
            pair_copy(phase, i).start()

        def for_own(i):
            if phase == 0:
                cov_copy(1, i).wait()
            part = project(vector, mine(i))
            pair_copy(phase, i).wait_recv()
            return part + pair_recv[phase, i]

        def send_own(i):
            send[i] = for_own(i).astype(send.dtype)
            rs_copy(phase, send, recv, i).start()

        def both(i, carry):
            send_own(i)
            for_sibling(i + 2)
            return carry

        for_sibling(0)
        for_sibling(1)
        lax.fori_loop(0, chips - 2, both, 0)
        send_own(chips - 2)

        def add(i, total):
            rs_copy(phase, send, recv, i).wait_recv()
            return total + recv[i].astype(jnp.float32)

        return lax.fori_loop(0, chips - 1, add, for_own(chips - 1))

    def ag_copy(phase, s):
        peer = sibling if s is None else chip_after(s) * 2 + core
        slot = 0 if s is None else s
        return pltpu.make_async_remote_copy(
            src_ref=share_send.at[phase], dst_ref=share_recv.at[phase, slot],
            send_sem=ag_ssem.at[phase, slot], recv_sem=ag_rsem.at[phase, slot],
            device_id={"col": peer}, device_id_type=MESH,
        )

    def forward(phase, s):
        return pltpu.make_async_remote_copy(
            src_ref=share_recv.at[phase, s], dst_ref=pass_recv.at[phase, s],
            send_sem=pass_ssem.at[phase, s], recv_sem=pass_rsem.at[phase, s],
            device_id={"col": sibling}, device_id_type=MESH,
        )

    def row_copy(phase, t, slot):
        return pltpu.make_async_remote_copy(
            src_ref=row_buf.at[phase, my_row], dst_ref=row_buf.at[phase, slot],
            send_sem=row_ssem.at[phase, t], recv_sem=row_rsem.at[phase, t],
            device_id={"row": lax.rem(my_row + t, rows)}, device_id_type=MESH,
        )

    def back_project(phase, values, meanwhile=None):
        share_send[phase] = values

        ag_copy(phase, None).start()

        def send(s, carry):
            ag_copy(phase, s).start()
            return carry

        lax.fori_loop(1, chips, send, 0)

        def term(block_values, block):
            return jnp.dot(block_values, cov[block], preferred_element_type=jnp.float32)

        def direct(s):
            ag_copy(phase, s).wait_recv()
            forward(phase, s).start()
            return term(share_recv[phase, s], chip_before(s) * 2 + core)

        def passed(s):
            forward(phase, s).wait_recv()
            return term(pass_recv[phase, s], chip_before(s) * 2 + 1 - core)

        def both(s, total):
            return total + direct(s + 1) + passed(s)

        total = term(values, me)
        ag_copy(phase, None).wait_recv()
        total = total + term(share_recv[phase, 0], sibling) + direct(1)
        total = lax.fori_loop(1, chips - 1, both, total)
        if meanwhile is not None:
            meanwhile()
        row_buf[phase, my_row] = total + passed(chips - 1)

        def send_row(t, carry):
            row_copy(phase, t, my_row).start()
            return carry

        def wait_row(t, carry):
            row_copy(phase, t, lax.rem(my_row + rows - t, rows)).wait_recv()
            return carry

        lax.fori_loop(1, rows, send_row, 0)
        lax.fori_loop(1, rows, wait_row, 0)
        total = row_buf[phase, 0]
        for r in range(1, rows):
            total = total + row_buf[phase, r]
        return total

    def dot_copy(phase, j):
        return pltpu.make_async_remote_copy(
            src_ref=dot_send.at[phase], dst_ref=dot_recv.at[phase, j],
            send_sem=dot_ssem.at[phase, j], recv_sem=dot_rsem.at[phase, j],
            device_id={"col": target(j)}, device_id_type=MESH,
        )

    def send_dots(phase, *tiles):
        for k, tile in enumerate(tiles):
            dot_send[phase, k] = tile

        def send(j, carry):
            dot_copy(phase, j).start()
            return carry

        lax.fori_loop(1, n, send, 0)

    def take_dots(phase, tiles):
        def add(j, totals):
            dot_copy(phase, j).wait_recv()
            return tuple(total + dot_recv[phase, j, k] for k, total in enumerate(totals))

        totals = lax.fori_loop(1, n, add, tuple(dot_send[phase, k] for k in range(tiles)))
        return [jnp.sum(total, keepdims=True) for total in totals]

    def curve_copy(phase, t, slot):
        return pltpu.make_async_remote_copy(
            src_ref=curve_buf.at[phase, my_row], dst_ref=curve_buf.at[phase, slot],
            send_sem=curve_ssem.at[phase, t], recv_sem=curve_rsem.at[phase, t],
            device_id={"row": lax.rem(my_row + t, rows)}, device_id_type=MESH,
        )

    def send_curve(phase, tile):
        curve_buf[phase, my_row] = tile

        def send(t, carry):
            curve_copy(phase, t, my_row).start()
            return carry

        lax.fori_loop(1, rows, send, 0)

    def take_curve(phase):
        def wait(t, carry):
            curve_copy(phase, t, lax.rem(my_row + rows - t, rows)).wait_recv()
            return carry

        lax.fori_loop(1, rows, wait, 0)
        total = curve_buf[phase, 0]
        for r in range(1, rows):
            total = total + curve_buf[phase, r]
        return total

    weights = weights_ref[...]
    logits = reduce_users(0, weights, logit_send, logit_recv)
    exponent = jnp.exp(logits)
    shares = exponent / jnp.sum(exponent, axis=0, keepdims=True)
    label = labels_ref[...]
    indicator = (label == lax.broadcasted_iota(jnp.int32, (classes, own), 0)).astype(jnp.float32)
    misfit = (shares - indicator).astype(jnp.bfloat16)
    gradient = back_project(0, misfit) / user_total + RIDGE_WEIGHT * weights
    gradient_ref[...] = gradient
    counted = count * shares

    residual = -gradient
    direction = residual
    newton_step = jnp.zeros_like(residual)
    norm_now = step_size = image = residual_response = direction_response = None
    for iteration in range(ITERS):
        last = iteration + 1 == ITERS
        vector = direction if iteration == 0 else image
        response = reduce_users(
            iteration + 1, vector, resp_send.at[iteration], resp_recv.at[iteration]
        )
        if iteration == 0:
            residual_response = direction_response = response
        else:
            (norm_new,) = take_dots(2 * iteration - 1, 1)
            ratio = norm_new / norm_now
            direction = residual + ratio * direction
            norm_now = norm_new
            residual_response = residual_response - step_size * response
            direction_response = residual_response + ratio * direction_response
        centred = direction_response - jnp.sum(shares * direction_response, axis=0, keepdims=True)
        weighted = (counted * centred).astype(jnp.bfloat16)
        send_curve(iteration, fold(weighted.astype(jnp.float32) * direction_response))
        square = fold(direction * direction)

        def pass_curve():
            tiles = [take_curve(iteration) / sub_total + RIDGE_WEIGHT * square]
            send_dots(2 * iteration, *(tiles + [square] if iteration == 0 else tiles))

        if last:
            pass_curve()
        else:
            image = back_project(iteration + 1, weighted, pass_curve) / sub_total + RIDGE_WEIGHT * direction
        if iteration == 0:
            curve, norm_now = take_dots(0, 2)
        else:
            (curve,) = take_dots(2 * iteration, 1)
        step_size = norm_now / curve
        newton_step = newton_step + step_size * direction
        if not last:
            residual = residual - step_size * image
            send_dots(2 * iteration + 1, fold(residual * residual))
    step_ref[...] = newton_step

    def drain_pair(i, carry):
        for phase in range(ITERS + 1):
            pair_copy(phase, i).wait_send()
        return carry

    def drain_chip(s, carry):
        rs_copy(0, logit_send, logit_recv, s - 1).wait_send()
        for phase in range(ITERS):
            rs_copy(phase + 1, resp_send.at[phase], resp_recv.at[phase], s - 1).wait_send()
        for phase in range(ITERS):
            ag_copy(phase, s).wait_send()
            forward(phase, s).wait_send()
        return carry

    def drain_col(j, carry):
        for phase in range(2 * ITERS - 1):
            dot_copy(phase, j).wait_send()
        return carry

    def drain_row(t, carry):
        for phase in range(ITERS):
            row_copy(phase, t, my_row).wait_send()
            curve_copy(phase, t, my_row).wait_send()
        return carry

    for phase in range(ITERS):
        ag_copy(phase, None).wait_send()
    lax.fori_loop(0, chips, drain_pair, 0)
    lax.fori_loop(1, chips, drain_chip, 0)
    lax.fori_loop(1, n, drain_col, 0)
    lax.fori_loop(1, rows, drain_row, 0)


def body(covariates, labels, weights, sample_index):
    users, width = covariates.shape
    n, rows = lax.axis_size("col"), lax.axis_size("row")
    own, chips = users // n, n // 2
    classes = weights.shape[0]
    sub = sample_index.shape[0]
    dots = 2 * ITERS - 1
    dma = pltpu.SemaphoreType.DMA
    out = pl.pallas_call(
        functools.partial(kernel, n, rows, users * rows, sub * rows),
        out_shape=[jax.ShapeDtypeStruct((classes, width), jnp.float32)] * 2,
        in_specs=[pl.BlockSpec(memory_space=pltpu.HBM)] * 4,
        out_specs=[pl.BlockSpec(memory_space=pltpu.VMEM)] * 2,
        scratch_shapes=[
            pltpu.VMEM((n, own, width), jnp.bfloat16),
            pltpu.VMEM((1, own), jnp.int32),
            pltpu.VMEM((classes, width), jnp.float32),
            pltpu.VMEM((1, sub), jnp.int32),
            pltpu.VMEM((ITERS + 1, chips, classes, own), jnp.float32),
            pltpu.VMEM((ITERS + 1, chips, classes, own), jnp.float32),
            pltpu.VMEM((chips, classes, own), jnp.float32),
            pltpu.VMEM((chips, classes, own), jnp.float32),
            pltpu.VMEM((ITERS, chips, classes, own), jnp.bfloat16),
            pltpu.VMEM((ITERS, chips, classes, own), jnp.bfloat16),
            pltpu.VMEM((ITERS, classes, own), jnp.bfloat16),
            pltpu.VMEM((ITERS, chips, classes, own), jnp.bfloat16),
            pltpu.VMEM((ITERS, chips, classes, own), jnp.bfloat16),
            pltpu.VMEM((ITERS, rows, classes, width), jnp.float32),
            pltpu.VMEM((ITERS, rows, 8, LANES), jnp.float32),
            pltpu.VMEM((dots, 2, 8, LANES), jnp.float32),
            pltpu.VMEM((dots, n, 2, 8, LANES), jnp.float32),
            dma((2, chips)), dma((3,)),
            dma((ITERS + 1, chips)), dma((ITERS + 1, chips)),
            dma((ITERS + 1, chips)), dma((ITERS + 1, chips)),
            dma((ITERS, chips)), dma((ITERS, chips)),
            dma((ITERS, chips)), dma((ITERS, chips)),
            dma((ITERS, rows)), dma((ITERS, rows)),
            dma((ITERS, rows)), dma((ITERS, rows)),
            dma((dots, n)), dma((dots, n)),
        ],
        compiler_params=pltpu.CompilerParams(
            collective_id=0, has_side_effects=True, vmem_limit_bytes=60 * 1024 * 1024
        ),
        name="newton_step",
    )(
        covariates.reshape(n, own, width), labels.reshape(n, 1, own), weights, sample_index.reshape(1, sub)
    )
    return tuple(out)


def solution(mesh):
    in_specs = (P("row", "col"), P("row"), P(None, "col"), P("row"))
    out_specs = (P(None, "col"), P(None, "col"))
    return jax.shard_map(body, mesh=mesh, in_specs=in_specs, out_specs=out_specs, check_vma=False)
```

```python
import functools

import jax
import jax.numpy as jnp
from jax import lax
from jax.experimental import pallas as pl
from jax.experimental.pallas import tpu as pltpu
from jax.sharding import PartitionSpec as P

ITERS = 2
RIDGE_WEIGHT = 0.004
LANES = 128
UNROLL = 8
MESH = pl.DeviceIdType.MESH


def fold(value):
    value = value[:8] + value[8:]
    total = value[:, :LANES]
    for start in range(LANES, value.shape[1], LANES):
        total = total + value[:, start:start + LANES]
    return total


def loop(first, end, step, carry):
    if end - first > UNROLL:
        return lax.fori_loop(first, end, step, carry)
    for i in range(first, end):
        carry = step(i, carry)
    return carry


def kernel(
    n, rows, user_total, sub_total,
    cov_hbm, labels_hbm, weights_hbm, index_hbm, gradient_ref, step_ref,
    cov, labels_ref, weights_ref, index_ref, pair_send, pair_recv, logit_send, logit_recv, resp_send, resp_recv,
    share_send, share_recv, pass_recv, row_buf, curve_buf, dot_send, dot_recv,
    cov_sem, small_sem, pair_ssem, pair_rsem, rs_ssem, rs_rsem, ag_ssem, ag_rsem, pass_ssem, pass_rsem,
    row_ssem, row_rsem, curve_ssem, curve_rsem, dot_ssem, dot_rsem,
):
    me = lax.axis_index("col")
    my_row = lax.axis_index("row")
    chips = n // 2
    own = cov.shape[1]
    classes = weights_ref.shape[0]

    chip, core = me // 2, lax.rem(me, 2)
    sibling = chip * 2 + 1 - core

    def target(j):
        return lax.rem(me + j, n)

    def chip_after(s):
        return lax.rem(chip + s, chips)

    def chip_before(s):
        return lax.rem(chip + chips - s, chips)

    def theirs(i):
        return chip_after(chips - 1 - i) * 2 + 1 - core

    def mine(i):
        return chip_after(chips - 1 - i) * 2 + core

    def cov_copy(side, i):
        block = theirs(i) if side == 0 else mine(i)
        return pltpu.make_async_copy(cov_hbm.at[block], cov.at[block], cov_sem.at[side, i])

    small_copies = [
        pltpu.make_async_copy(weights_hbm, weights_ref, small_sem.at[0]),
        pltpu.make_async_copy(index_hbm, index_ref, small_sem.at[1]),
        pltpu.make_async_copy(labels_hbm.at[me], labels_ref, small_sem.at[2]),
    ]
    for copy in small_copies:
        copy.start()

    def start_cov(i, carry):
        cov_copy(0, i).start()
        cov_copy(1, i).start()
        return carry

    loop(0, chips, start_cov, 0)

    barrier = pltpu.get_barrier_semaphore()

    def greet_col(j, carry):
        pl.semaphore_signal(barrier, inc=1, device_id={"col": target(j)}, device_id_type=MESH)
        return carry

    def greet_row(t, carry):
        pl.semaphore_signal(
            barrier, inc=1, device_id={"row": lax.rem(my_row + t, rows)}, device_id_type=MESH
        )
        return carry

    loop(1, n, greet_col, 0)
    loop(1, rows, greet_row, 0)

    for copy in small_copies:
        copy.wait()

    groups = own // LANES
    padded = max(16, groups)
    within = index_ref[...] - my_row * (n * own) - me * own
    lane = jnp.bitwise_and(within, LANES - 1)
    group = jnp.right_shift(within - lane, 7)
    group_hot = (lax.broadcasted_iota(jnp.int32, (padded, within.shape[1]), 0) == group)
    lane_hot = (lax.broadcasted_iota(jnp.int32, (LANES, within.shape[1]), 0) == lane)
    counts = lax.dot_general(
        group_hot.astype(jnp.float32).astype(jnp.bfloat16), lane_hot.astype(jnp.float32).astype(jnp.bfloat16),
        (((1,), (1,)), ((), ())), preferred_element_type=jnp.float32,
    )
    count = jnp.concatenate([counts[g:g + 1] for g in range(groups)], axis=1)

    pl.semaphore_wait(barrier, n - 1 + rows - 1)

    def pair_copy(phase, i):
        return pltpu.make_async_remote_copy(
            src_ref=pair_send.at[phase, i], dst_ref=pair_recv.at[phase, i],
            send_sem=pair_ssem.at[phase, i], recv_sem=pair_rsem.at[phase, i],
            device_id={"col": sibling}, device_id_type=MESH,
        )

    def rs_copy(phase, send, recv, i):
        return pltpu.make_async_remote_copy(
            src_ref=send.at[i], dst_ref=recv.at[i],
            send_sem=rs_ssem.at[phase, i], recv_sem=rs_rsem.at[phase, i],
            device_id={"col": mine(i)}, device_id_type=MESH,
        )

    def project(vector, block):
        return lax.dot_general(
            vector, cov[block], (((1,), (1,)), ((), ())), preferred_element_type=jnp.float32
        )

    def reduce_users(phase, vector, send, recv):
        vector = vector.astype(jnp.bfloat16)

        def for_sibling(i):
            if phase == 0:
                cov_copy(0, i).wait()
            pair_send[phase, i] = project(vector, theirs(i))
            pair_copy(phase, i).start()

        def for_own(i):
            if phase == 0:
                cov_copy(1, i).wait()
            part = project(vector, mine(i))
            pair_copy(phase, i).wait_recv()
            return part + pair_recv[phase, i]

        def send_own(i):
            send[i] = for_own(i).astype(send.dtype)
            rs_copy(phase, send, recv, i).start()

        def both(i, carry):
            send_own(i)
            for_sibling(i + 2)
            return carry

        for_sibling(0)
        for_sibling(1)
        loop(0, chips - 2, both, 0)
        send_own(chips - 2)

        def add(i, total):
            rs_copy(phase, send, recv, i).wait_recv()
            return total + recv[i].astype(jnp.float32)

        return loop(0, chips - 1, add, for_own(chips - 1))

    def ag_copy(phase, s):
        peer = sibling if s is None else chip_after(s) * 2 + core
        slot = 0 if s is None else s
        return pltpu.make_async_remote_copy(
            src_ref=share_send.at[phase], dst_ref=share_recv.at[phase, slot],
            send_sem=ag_ssem.at[phase, slot], recv_sem=ag_rsem.at[phase, slot],
            device_id={"col": peer}, device_id_type=MESH,
        )

    def forward(phase, s):
        return pltpu.make_async_remote_copy(
            src_ref=share_recv.at[phase, s], dst_ref=pass_recv.at[phase, s],
            send_sem=pass_ssem.at[phase, s], recv_sem=pass_rsem.at[phase, s],
            device_id={"col": sibling}, device_id_type=MESH,
        )

    def row_copy(phase, t, slot):
        return pltpu.make_async_remote_copy(
            src_ref=row_buf.at[phase, my_row], dst_ref=row_buf.at[phase, slot],
            send_sem=row_ssem.at[phase, t], recv_sem=row_rsem.at[phase, t],
            device_id={"row": lax.rem(my_row + t, rows)}, device_id_type=MESH,
        )

    def back_project(phase, values, meanwhile=None):
        share_send[phase] = values

        ag_copy(phase, None).start()

        def send(s, carry):
            ag_copy(phase, s).start()
            return carry

        loop(1, chips, send, 0)

        def term(block_values, block):
            return jnp.dot(block_values, cov[block], preferred_element_type=jnp.float32)

        def direct(s):
            ag_copy(phase, s).wait_recv()
            forward(phase, s).start()
            return term(share_recv[phase, s], chip_before(s) * 2 + core)

        def passed(s):
            forward(phase, s).wait_recv()
            return term(pass_recv[phase, s], chip_before(s) * 2 + 1 - core)

        def both(s, total):
            return total + direct(s + 1) + passed(s)

        total = term(values, me)
        ag_copy(phase, None).wait_recv()
        total = total + term(share_recv[phase, 0], sibling) + direct(1)
        total = loop(1, chips - 1, both, total)
        if meanwhile is not None:
            meanwhile()
        row_buf[phase, my_row] = total + passed(chips - 1)

        def send_row(t, carry):
            row_copy(phase, t, my_row).start()
            return carry

        def wait_row(t, carry):
            row_copy(phase, t, lax.rem(my_row + rows - t, rows)).wait_recv()
            return carry

        loop(1, rows, send_row, 0)
        loop(1, rows, wait_row, 0)
        total = row_buf[phase, 0]
        for r in range(1, rows):
            total = total + row_buf[phase, r]
        return total

    def dot_copy(phase, j):
        return pltpu.make_async_remote_copy(
            src_ref=dot_send.at[phase], dst_ref=dot_recv.at[phase, j],
            send_sem=dot_ssem.at[phase, j], recv_sem=dot_rsem.at[phase, j],
            device_id={"col": target(j)}, device_id_type=MESH,
        )

    def send_dots(phase, *tiles):
        for k, tile in enumerate(tiles):
            dot_send[phase, k] = tile

        def send(j, carry):
            dot_copy(phase, j).start()
            return carry

        loop(1, n, send, 0)

    def take_dots(phase, tiles):
        def add(j, totals):
            dot_copy(phase, j).wait_recv()
            return tuple(total + dot_recv[phase, j, k] for k, total in enumerate(totals))

        totals = loop(1, n, add, tuple(dot_send[phase, k] for k in range(tiles)))
        return [jnp.sum(total, keepdims=True) for total in totals]

    def curve_copy(phase, t, slot):
        return pltpu.make_async_remote_copy(
            src_ref=curve_buf.at[phase, my_row], dst_ref=curve_buf.at[phase, slot],
            send_sem=curve_ssem.at[phase, t], recv_sem=curve_rsem.at[phase, t],
            device_id={"row": lax.rem(my_row + t, rows)}, device_id_type=MESH,
        )

    def send_curve(phase, tile):
        curve_buf[phase, my_row] = tile

        def send(t, carry):
            curve_copy(phase, t, my_row).start()
            return carry

        loop(1, rows, send, 0)

    def take_curve(phase):
        def wait(t, carry):
            curve_copy(phase, t, lax.rem(my_row + rows - t, rows)).wait_recv()
            return carry

        loop(1, rows, wait, 0)
        total = curve_buf[phase, 0]
        for r in range(1, rows):
            total = total + curve_buf[phase, r]
        return total

    weights = weights_ref[...]
    logits = reduce_users(0, weights, logit_send, logit_recv)
    exponent = jnp.exp(logits)
    shares = exponent / jnp.sum(exponent, axis=0, keepdims=True)
    label = labels_ref[...]
    indicator = (label == lax.broadcasted_iota(jnp.int32, (classes, own), 0)).astype(jnp.float32)
    misfit = (shares - indicator).astype(jnp.bfloat16)
    gradient = back_project(0, misfit) / user_total + RIDGE_WEIGHT * weights
    gradient_ref[...] = gradient
    counted = count * shares

    residual = -gradient
    direction = residual
    newton_step = jnp.zeros_like(residual)
    norm_now = step_size = image = residual_response = direction_response = None
    for iteration in range(ITERS):
        last = iteration + 1 == ITERS
        vector = direction if iteration == 0 else image
        response = reduce_users(
            iteration + 1, vector, resp_send.at[iteration], resp_recv.at[iteration]
        )
        if iteration == 0:
            residual_response = direction_response = response
        else:
            (norm_new,) = take_dots(2 * iteration - 1, 1)
            ratio = norm_new / norm_now
            direction = residual + ratio * direction
            norm_now = norm_new
            residual_response = residual_response - step_size * response
            direction_response = residual_response + ratio * direction_response
        centred = direction_response - jnp.sum(shares * direction_response, axis=0, keepdims=True)
        weighted = (counted * centred).astype(jnp.bfloat16)
        send_curve(iteration, fold(weighted.astype(jnp.float32) * direction_response))
        square = fold(direction * direction)

        def pass_curve():
            tiles = [take_curve(iteration) / sub_total + RIDGE_WEIGHT * square]
            send_dots(2 * iteration, *(tiles + [square] if iteration == 0 else tiles))

        if last:
            pass_curve()
        else:
            image = back_project(iteration + 1, weighted, pass_curve) / sub_total + RIDGE_WEIGHT * direction
        if iteration == 0:
            curve, norm_now = take_dots(0, 2)
        else:
            (curve,) = take_dots(2 * iteration, 1)
        step_size = norm_now / curve
        newton_step = newton_step + step_size * direction
        if not last:
            residual = residual - step_size * image
            send_dots(2 * iteration + 1, fold(residual * residual))
    step_ref[...] = newton_step

    def drain_pair(i, carry):
        for phase in range(ITERS + 1):
            pair_copy(phase, i).wait_send()
        return carry

    def drain_chip(s, carry):
        rs_copy(0, logit_send, logit_recv, s - 1).wait_send()
        for phase in range(ITERS):
            rs_copy(phase + 1, resp_send.at[phase], resp_recv.at[phase], s - 1).wait_send()
        for phase in range(ITERS):
            ag_copy(phase, s).wait_send()
            forward(phase, s).wait_send()
        return carry

    def drain_col(j, carry):
        for phase in range(2 * ITERS - 1):
            dot_copy(phase, j).wait_send()
        return carry

    def drain_row(t, carry):
        for phase in range(ITERS):
            row_copy(phase, t, my_row).wait_send()
            curve_copy(phase, t, my_row).wait_send()
        return carry

    for phase in range(ITERS):
        ag_copy(phase, None).wait_send()
    loop(0, chips, drain_pair, 0)
    loop(1, chips, drain_chip, 0)
    loop(1, n, drain_col, 0)
    loop(1, rows, drain_row, 0)


def body(covariates, labels, weights, sample_index):
    users, width = covariates.shape
    n, rows = lax.axis_size("col"), lax.axis_size("row")
    own, chips = users // n, n // 2
    classes = weights.shape[0]
    sub = sample_index.shape[0]
    dots = 2 * ITERS - 1
    dma = pltpu.SemaphoreType.DMA
    out = pl.pallas_call(
        functools.partial(kernel, n, rows, users * rows, sub * rows),
        out_shape=[jax.ShapeDtypeStruct((classes, width), jnp.float32)] * 2,
        in_specs=[pl.BlockSpec(memory_space=pltpu.HBM)] * 4,
        out_specs=[pl.BlockSpec(memory_space=pltpu.VMEM)] * 2,
        scratch_shapes=[
            pltpu.VMEM((n, own, width), jnp.bfloat16),
            pltpu.VMEM((1, own), jnp.int32),
            pltpu.VMEM((classes, width), jnp.float32),
            pltpu.VMEM((1, sub), jnp.int32),
            pltpu.VMEM((ITERS + 1, chips, classes, own), jnp.float32),
            pltpu.VMEM((ITERS + 1, chips, classes, own), jnp.float32),
            pltpu.VMEM((chips, classes, own), jnp.float32),
            pltpu.VMEM((chips, classes, own), jnp.float32),
            pltpu.VMEM((ITERS, chips, classes, own), jnp.bfloat16),
            pltpu.VMEM((ITERS, chips, classes, own), jnp.bfloat16),
            pltpu.VMEM((ITERS, classes, own), jnp.bfloat16),
            pltpu.VMEM((ITERS, chips, classes, own), jnp.bfloat16),
            pltpu.VMEM((ITERS, chips, classes, own), jnp.bfloat16),
            pltpu.VMEM((ITERS, rows, classes, width), jnp.float32),
            pltpu.VMEM((ITERS, rows, 8, LANES), jnp.float32),
            pltpu.VMEM((dots, 2, 8, LANES), jnp.float32),
            pltpu.VMEM((dots, n, 2, 8, LANES), jnp.float32),
            dma((2, chips)), dma((3,)),
            dma((ITERS + 1, chips)), dma((ITERS + 1, chips)),
            dma((ITERS + 1, chips)), dma((ITERS + 1, chips)),
            dma((ITERS, chips)), dma((ITERS, chips)),
            dma((ITERS, chips)), dma((ITERS, chips)),
            dma((ITERS, rows)), dma((ITERS, rows)),
            dma((ITERS, rows)), dma((ITERS, rows)),
            dma((dots, n)), dma((dots, n)),
        ],
        compiler_params=pltpu.CompilerParams(
            collective_id=0, has_side_effects=True, vmem_limit_bytes=60 * 1024 * 1024
        ),
        name="newton_step",
    )(
        covariates.reshape(n, own, width), labels.reshape(n, 1, own), weights, sample_index.reshape(1, sub)
    )
    return tuple(out)


def solution(mesh):
    in_specs = (P("row", "col"), P("row"), P(None, "col"), P("row"))
    out_specs = (P(None, "col"), P(None, "col"))
    return jax.shard_map(body, mesh=mesh, in_specs=in_specs, out_specs=out_specs, check_vma=False)
```

```python
import functools

import jax
import jax.numpy as jnp
from jax import lax
from jax.experimental import pallas as pl
from jax.experimental.pallas import tpu as pltpu
from jax.sharding import PartitionSpec as P

ITERS = 2
RIDGE_WEIGHT = 0.004
LANES = 128
MESH = pl.DeviceIdType.MESH


def fold(value):
    value = value[:8] + value[8:]
    total = value[:, :LANES]
    for start in range(LANES, value.shape[1], LANES):
        total = total + value[:, start:start + LANES]
    return total


def kernel(
    n, rows, user_total, sub_total,
    cov_hbm, labels_hbm, weights_hbm, index_hbm, gradient_ref, step_ref,
    cov, labels_ref, weights_ref, index_ref, pair_send, pair_recv, logit_send, logit_recv, resp_send, resp_recv,
    chip_sum, got, row_buf, curve_buf, dot_send, dot_recv,
    cov_sem, small_sem, pair_ssem, pair_rsem, rs_ssem, rs_rsem, ag_ssem, ag_rsem, pass_ssem, pass_rsem,
    row_ssem, row_rsem, curve_ssem, curve_rsem, dot_ssem, dot_rsem,
):
    me = lax.axis_index("col")
    my_row = lax.axis_index("row")
    chips = n // 2
    own = cov.shape[1]
    classes = weights_ref.shape[0]

    chip, core = me // 2, lax.rem(me, 2)
    sibling = chip * 2 + 1 - core

    def target(j):
        return lax.rem(me + j, n)

    def chip_after(s):
        return lax.rem(chip + s, chips)

    def chip_before(s):
        return lax.rem(chip + chips - s, chips)

    def mine(i):
        return chip_after(chips - 1 - i) * 2 + core

    def send_order(u):
        first, last, odd = (n - 1 - u) // (n - 1), u // (n - 1), lax.rem(u, 2)
        side = 1 - first - odd * (1 - last)
        i = odd * (1 - last) * ((u + 1) // 2) + last * (chips - 1) + (1 - odd) * (1 - first) * ((u + first) // 2 - 1 + first)
        return side, i

    def take_order(u):
        last, odd, late = u // (n - 1), lax.rem(u, 2), (u + n - 3) // n
        side = late * (last + (1 - odd)) + (1 - late) * odd
        s = late * (last * (chips - 1) + odd * (1 - last) * ((u + 1) // 2) + (1 - odd) * (u // 2 - 1)) + (1 - late) * (u // 2)
        return side, s

    def send_block(side, i):
        return chip_after(chips - 1 - i) * 2 + side * core + (1 - side) * (1 - core)

    def cov_copy(u):
        block = send_block(*send_order(u))
        return pltpu.make_async_copy(cov_hbm.at[block], cov.at[block], cov_sem.at[u])

    small_copies = [
        pltpu.make_async_copy(weights_hbm, weights_ref, small_sem.at[0]),
        pltpu.make_async_copy(index_hbm, index_ref, small_sem.at[1]),
        pltpu.make_async_copy(labels_hbm.at[me], labels_ref, small_sem.at[2]),
    ]
    for copy in small_copies:
        copy.start()

    def start_cov(u, carry):
        cov_copy(u).start()
        return carry

    lax.fori_loop(0, n, start_cov, 0)

    barrier = pltpu.get_barrier_semaphore()

    def greet_col(j, carry):
        pl.semaphore_signal(barrier, inc=1, device_id={"col": target(j)}, device_id_type=MESH)
        return carry

    def greet_row(t, carry):
        pl.semaphore_signal(
            barrier, inc=1, device_id={"row": lax.rem(my_row + t, rows)}, device_id_type=MESH
        )
        return carry

    lax.fori_loop(1, n, greet_col, 0)
    lax.fori_loop(1, rows, greet_row, 0)

    for copy in small_copies:
        copy.wait()

    groups = own // LANES
    padded = max(16, groups)
    within = index_ref[...] - my_row * (n * own) - me * own
    lane = jnp.bitwise_and(within, LANES - 1)
    group = jnp.right_shift(within - lane, 7)
    group_hot = (lax.broadcasted_iota(jnp.int32, (padded, within.shape[1]), 0) == group)
    lane_hot = (lax.broadcasted_iota(jnp.int32, (LANES, within.shape[1]), 0) == lane)
    counts = lax.dot_general(
        group_hot.astype(jnp.float32).astype(jnp.bfloat16), lane_hot.astype(jnp.float32).astype(jnp.bfloat16),
        (((1,), (1,)), ((), ())), preferred_element_type=jnp.float32,
    )
    count = jnp.concatenate([counts[g:g + 1] for g in range(groups)], axis=1)

    pl.semaphore_wait(barrier, n - 1 + rows - 1)

    def pair_copy(phase, i):
        return pltpu.make_async_remote_copy(
            src_ref=pair_send.at[phase, i], dst_ref=pair_recv.at[phase, i],
            send_sem=pair_ssem.at[phase, i], recv_sem=pair_rsem.at[phase, i],
            device_id={"col": sibling}, device_id_type=MESH,
        )

    def rs_copy(phase, send, recv, i):
        return pltpu.make_async_remote_copy(
            src_ref=send.at[i], dst_ref=recv.at[i],
            send_sem=rs_ssem.at[phase, i], recv_sem=rs_rsem.at[phase, i],
            device_id={"col": mine(i)}, device_id_type=MESH,
        )

    def project(vector, block):
        return lax.dot_general(
            vector, cov[block], (((1,), (1,)), ((), ())), preferred_element_type=jnp.float32
        )

    def reduce_users(phase, vector, send, recv):
        vector = vector.astype(jnp.bfloat16)

        def one(u, carry):
            side, i = send_order(u)
            if phase == 0:
                cov_copy(u).wait()
            part = project(vector, send_block(side, i))

            @pl.when(side == 0)
            def _():
                pair_send[phase, i] = part
                pair_copy(phase, i).start()

            @pl.when(side == 1)
            def _():
                pair_copy(phase, i).wait_recv()
                chip_sum[...] = part + pair_recv[phase, i]

                @pl.when(i < chips - 1)
                def _():
                    send[i] = chip_sum[...].astype(send.dtype)
                    rs_copy(phase, send, recv, i).start()

            return carry

        lax.fori_loop(0, n, one, 0)

        def add(i, total):
            rs_copy(phase, send, recv, i).wait_recv()
            return total + recv[i].astype(jnp.float32)

        return lax.fori_loop(0, chips - 1, add, chip_sum[...])

    def ag_copy(phase, s):
        return pltpu.make_async_remote_copy(
            src_ref=got.at[phase, 0, 0], dst_ref=got.at[phase, 0, s],
            send_sem=ag_ssem.at[phase, s], recv_sem=ag_rsem.at[phase, s],
            device_id={"col": chip_after(s) * 2 + core}, device_id_type=MESH,
        )

    def forward(phase, s):
        return pltpu.make_async_remote_copy(
            src_ref=got.at[phase, 0, s], dst_ref=got.at[phase, 1, s],
            send_sem=pass_ssem.at[phase, s], recv_sem=pass_rsem.at[phase, s],
            device_id={"col": sibling}, device_id_type=MESH,
        )

    def row_copy(phase, t, slot):
        return pltpu.make_async_remote_copy(
            src_ref=row_buf.at[phase, my_row], dst_ref=row_buf.at[phase, slot],
            send_sem=row_ssem.at[phase, t], recv_sem=row_rsem.at[phase, t],
            device_id={"row": lax.rem(my_row + t, rows)}, device_id_type=MESH,
        )

    def back_project(phase, values, meanwhile=None):
        got[phase, 0, 0] = values
        forward(phase, 0).start()

        def send(s, carry):
            ag_copy(phase, s).start()
            return carry

        lax.fori_loop(1, chips, send, 0)

        def add(u, total):
            side, s = take_order(u)

            @pl.when(side == 1)
            def _():
                forward(phase, s).wait_recv()

            @pl.when(jnp.logical_and(side == 0, s > 0))
            def _():
                ag_copy(phase, s).wait_recv()
                forward(phase, s).start()

            block = chip_before(s) * 2 + (1 - side) * core + side * (1 - core)
            return total + jnp.dot(got[phase, side, s], cov[block], preferred_element_type=jnp.float32)

        total = lax.fori_loop(0, n - 1, add, jnp.zeros(weights_ref.shape, jnp.float32))
        if meanwhile is not None:
            meanwhile()
        row_buf[phase, my_row] = add(n - 1, total)

        def send_row(t, carry):
            row_copy(phase, t, my_row).start()
            return carry

        def wait_row(t, carry):
            row_copy(phase, t, lax.rem(my_row + rows - t, rows)).wait_recv()
            return carry

        lax.fori_loop(1, rows, send_row, 0)
        lax.fori_loop(1, rows, wait_row, 0)
        total = row_buf[phase, 0]
        for r in range(1, rows):
            total = total + row_buf[phase, r]
        return total

    def dot_copy(phase, j):
        return pltpu.make_async_remote_copy(
            src_ref=dot_send.at[phase], dst_ref=dot_recv.at[phase, j],
            send_sem=dot_ssem.at[phase, j], recv_sem=dot_rsem.at[phase, j],
            device_id={"col": target(j)}, device_id_type=MESH,
        )

    def send_dots(phase, *tiles):
        for k, tile in enumerate(tiles):
            dot_send[phase, k] = tile

        def send(j, carry):
            dot_copy(phase, j).start()
            return carry

        lax.fori_loop(1, n, send, 0)

    def take_dots(phase, tiles):
        def add(j, totals):
            dot_copy(phase, j).wait_recv()
            return tuple(total + dot_recv[phase, j, k] for k, total in enumerate(totals))

        totals = lax.fori_loop(1, n, add, tuple(dot_send[phase, k] for k in range(tiles)))
        return [jnp.sum(total, keepdims=True) for total in totals]

    def curve_copy(phase, t, slot):
        return pltpu.make_async_remote_copy(
            src_ref=curve_buf.at[phase, my_row], dst_ref=curve_buf.at[phase, slot],
            send_sem=curve_ssem.at[phase, t], recv_sem=curve_rsem.at[phase, t],
            device_id={"row": lax.rem(my_row + t, rows)}, device_id_type=MESH,
        )

    def send_curve(phase, tile):
        curve_buf[phase, my_row] = tile

        def send(t, carry):
            curve_copy(phase, t, my_row).start()
            return carry

        lax.fori_loop(1, rows, send, 0)

    def take_curve(phase):
        def wait(t, carry):
            curve_copy(phase, t, lax.rem(my_row + rows - t, rows)).wait_recv()
            return carry

        lax.fori_loop(1, rows, wait, 0)
        total = curve_buf[phase, 0]
        for r in range(1, rows):
            total = total + curve_buf[phase, r]
        return total

    weights = weights_ref[...]
    logits = reduce_users(0, weights, logit_send, logit_recv)
    exponent = jnp.exp(logits)
    shares = exponent / jnp.sum(exponent, axis=0, keepdims=True)
    label = labels_ref[...]
    indicator = (label == lax.broadcasted_iota(jnp.int32, (classes, own), 0)).astype(jnp.float32)
    misfit = (shares - indicator).astype(jnp.bfloat16)
    gradient = back_project(0, misfit) / user_total + RIDGE_WEIGHT * weights
    gradient_ref[...] = gradient
    counted = count * shares

    residual = -gradient
    direction = residual
    newton_step = jnp.zeros_like(residual)
    norm_now = step_size = image = residual_response = direction_response = None
    for iteration in range(ITERS):
        last = iteration + 1 == ITERS
        vector = direction if iteration == 0 else image
        response = reduce_users(
            iteration + 1, vector, resp_send.at[iteration], resp_recv.at[iteration]
        )
        if iteration == 0:
            residual_response = direction_response = response
        else:
            (norm_new,) = take_dots(2 * iteration - 1, 1)
            ratio = norm_new / norm_now
            direction = residual + ratio * direction
            norm_now = norm_new
            residual_response = residual_response - step_size * response
            direction_response = residual_response + ratio * direction_response
        centred = direction_response - jnp.sum(shares * direction_response, axis=0, keepdims=True)
        weighted = (counted * centred).astype(jnp.bfloat16)
        send_curve(iteration, fold(weighted.astype(jnp.float32) * direction_response))
        square = fold(direction * direction)

        def pass_curve():
            tiles = [take_curve(iteration) / sub_total + RIDGE_WEIGHT * square]
            send_dots(2 * iteration, *(tiles + [square] if iteration == 0 else tiles))

        if last:
            pass_curve()
        else:
            image = back_project(iteration + 1, weighted, pass_curve) / sub_total + RIDGE_WEIGHT * direction
        if iteration == 0:
            curve, norm_now = take_dots(0, 2)
        else:
            (curve,) = take_dots(2 * iteration, 1)
        step_size = norm_now / curve
        newton_step = newton_step + step_size * direction
        if not last:
            residual = residual - step_size * image
            send_dots(2 * iteration + 1, fold(residual * residual))
    step_ref[...] = newton_step

    def drain_pair(i, carry):
        for phase in range(ITERS + 1):
            pair_copy(phase, i).wait_send()
        return carry

    def drain_chip(s, carry):
        rs_copy(0, logit_send, logit_recv, s - 1).wait_send()
        for phase in range(ITERS):
            rs_copy(phase + 1, resp_send.at[phase], resp_recv.at[phase], s - 1).wait_send()
        for phase in range(ITERS):
            ag_copy(phase, s).wait_send()
            forward(phase, s).wait_send()
        return carry

    def drain_col(j, carry):
        for phase in range(2 * ITERS - 1):
            dot_copy(phase, j).wait_send()
        return carry

    def drain_row(t, carry):
        for phase in range(ITERS):
            row_copy(phase, t, my_row).wait_send()
            curve_copy(phase, t, my_row).wait_send()
        return carry

    for phase in range(ITERS):
        forward(phase, 0).wait_send()
    lax.fori_loop(0, chips, drain_pair, 0)
    lax.fori_loop(1, chips, drain_chip, 0)
    lax.fori_loop(1, n, drain_col, 0)
    lax.fori_loop(1, rows, drain_row, 0)


def body(covariates, labels, weights, sample_index):
    users, width = covariates.shape
    n, rows = lax.axis_size("col"), lax.axis_size("row")
    own, chips = users // n, n // 2
    classes = weights.shape[0]
    sub = sample_index.shape[0]
    dots = 2 * ITERS - 1
    dma = pltpu.SemaphoreType.DMA
    out = pl.pallas_call(
        functools.partial(kernel, n, rows, users * rows, sub * rows),
        out_shape=[jax.ShapeDtypeStruct((classes, width), jnp.float32)] * 2,
        in_specs=[pl.BlockSpec(memory_space=pltpu.HBM)] * 4,
        out_specs=[pl.BlockSpec(memory_space=pltpu.VMEM)] * 2,
        scratch_shapes=[
            pltpu.VMEM((n, own, width), jnp.bfloat16),
            pltpu.VMEM((1, own), jnp.int32),
            pltpu.VMEM((classes, width), jnp.float32),
            pltpu.VMEM((1, sub), jnp.int32),
            pltpu.VMEM((ITERS + 1, chips, classes, own), jnp.float32),
            pltpu.VMEM((ITERS + 1, chips, classes, own), jnp.float32),
            pltpu.VMEM((chips, classes, own), jnp.float32),
            pltpu.VMEM((chips, classes, own), jnp.float32),
            pltpu.VMEM((ITERS, chips, classes, own), jnp.bfloat16),
            pltpu.VMEM((ITERS, chips, classes, own), jnp.bfloat16),
            pltpu.VMEM((classes, own), jnp.float32),
            pltpu.VMEM((ITERS, 2, chips, classes, own), jnp.bfloat16),
            pltpu.VMEM((ITERS, rows, classes, width), jnp.float32),
            pltpu.VMEM((ITERS, rows, 8, LANES), jnp.float32),
            pltpu.VMEM((dots, 2, 8, LANES), jnp.float32),
            pltpu.VMEM((dots, n, 2, 8, LANES), jnp.float32),
            dma((n,)), dma((3,)),
            dma((ITERS + 1, chips)), dma((ITERS + 1, chips)),
            dma((ITERS + 1, chips)), dma((ITERS + 1, chips)),
            dma((ITERS, chips)), dma((ITERS, chips)),
            dma((ITERS, chips)), dma((ITERS, chips)),
            dma((ITERS, rows)), dma((ITERS, rows)),
            dma((ITERS, rows)), dma((ITERS, rows)),
            dma((dots, n)), dma((dots, n)),
        ],
        compiler_params=pltpu.CompilerParams(
            collective_id=0, has_side_effects=True, vmem_limit_bytes=60 * 1024 * 1024
        ),
        name="newton_step",
    )(
        covariates.reshape(n, own, width), labels.reshape(n, 1, own), weights, sample_index.reshape(1, sub)
    )
    return tuple(out)


def solution(mesh):
    in_specs = (P("row", "col"), P("row"), P(None, "col"), P("row"))
    out_specs = (P(None, "col"), P(None, "col"))
    return jax.shard_map(body, mesh=mesh, in_specs=in_specs, out_specs=out_specs, check_vma=False)
```

```python
import functools

import jax
import jax.numpy as jnp
from jax import lax
from jax.experimental import pallas as pl
from jax.experimental.pallas import tpu as pltpu
from jax.sharding import PartitionSpec as P

ITERS = 2
RIDGE_WEIGHT = 0.004
LANES = 128
PARTS = 2
MESH = pl.DeviceIdType.MESH


def fold(value):
    value = value[:8] + value[8:]
    total = value[:, :LANES]
    for start in range(LANES, value.shape[1], LANES):
        total = total + value[:, start:start + LANES]
    return total


def kernel(
    n, rows, user_total, sub_total,
    cov_hbm, labels_hbm, weights_hbm, index_hbm, gradient_ref, step_ref,
    cov, labels_ref, weights_ref, index_ref, pair_send, pair_recv, logit_send, logit_recv, resp_send, resp_recv,
    chip_sum, got, row_buf, curve_buf, dot_send, dot_recv,
    cov_sem, small_sem, pair_ssem, pair_rsem, rs_ssem, rs_rsem, ag_ssem, ag_rsem, pass_ssem, pass_rsem,
    row_ssem, row_rsem, curve_ssem, curve_rsem, dot_ssem, dot_rsem,
):
    me = lax.axis_index("col")
    my_row = lax.axis_index("row")
    chips = n // 2
    own = cov.shape[1]
    half = own // PARTS
    classes = weights_ref.shape[0]

    chip, core = me // 2, lax.rem(me, 2)
    sibling = chip * 2 + 1 - core

    def target(j):
        return lax.rem(me + j, n)

    def chip_after(s):
        return lax.rem(chip + s, chips)

    def chip_before(s):
        return lax.rem(chip + chips - s, chips)

    def mine(i):
        return chip_after(chips - 1 - i) * 2 + core

    def send_order(u):
        first, last, odd = (n - 1 - u) // (n - 1), u // (n - 1), lax.rem(u, 2)
        side = 1 - first - odd * (1 - last)
        i = odd * (1 - last) * ((u + 1) // 2) + last * (chips - 1) + (1 - odd) * (1 - first) * ((u + first) // 2 - 1 + first)
        return side, i

    def take_order(u):
        last, odd, late = u // (n - 1), lax.rem(u, 2), (u + n - 3) // n
        side = late * (last + (1 - odd)) + (1 - late) * odd
        s = late * (last * (chips - 1) + odd * (1 - last) * ((u + 1) // 2) + (1 - odd) * (u // 2 - 1)) + (1 - late) * (u // 2)
        return side, s

    def send_block(side, i):
        return chip_after(chips - 1 - i) * 2 + side * core + (1 - side) * (1 - core)

    def users(h):
        return pl.ds(h * half, half)

    def cov_copy(u, h):
        block = send_block(*send_order(u))
        return pltpu.make_async_copy(
            cov_hbm.at[block, users(h)], cov.at[block, users(h)], cov_sem.at[h, u]
        )

    small_copies = [
        pltpu.make_async_copy(weights_hbm, weights_ref, small_sem.at[0]),
        pltpu.make_async_copy(index_hbm, index_ref, small_sem.at[1]),
        pltpu.make_async_copy(labels_hbm.at[me], labels_ref, small_sem.at[2]),
    ]
    for copy in small_copies:
        copy.start()

    for h in range(PARTS):

        def start_cov(u, carry):
            cov_copy(u, h).start()
            return carry

        lax.fori_loop(0, n, start_cov, 0)

    barrier = pltpu.get_barrier_semaphore()

    def greet_col(j, carry):
        pl.semaphore_signal(barrier, inc=1, device_id={"col": target(j)}, device_id_type=MESH)
        return carry

    def greet_row(t, carry):
        pl.semaphore_signal(
            barrier, inc=1, device_id={"row": lax.rem(my_row + t, rows)}, device_id_type=MESH
        )
        return carry

    lax.fori_loop(1, n, greet_col, 0)
    lax.fori_loop(1, rows, greet_row, 0)

    for copy in small_copies:
        copy.wait()

    groups = own // LANES
    padded = max(16, groups)
    within = index_ref[...] - my_row * (n * own) - me * own
    lane = jnp.bitwise_and(within, LANES - 1)
    group = jnp.right_shift(within - lane, 7)
    group_hot = (lax.broadcasted_iota(jnp.int32, (padded, within.shape[1]), 0) == group)
    lane_hot = (lax.broadcasted_iota(jnp.int32, (LANES, within.shape[1]), 0) == lane)
    counts = lax.dot_general(
        group_hot.astype(jnp.float32).astype(jnp.bfloat16), lane_hot.astype(jnp.float32).astype(jnp.bfloat16),
        (((1,), (1,)), ((), ())), preferred_element_type=jnp.float32,
    )
    count = jnp.concatenate([counts[g:g + 1] for g in range(groups)], axis=1)

    pl.semaphore_wait(barrier, n - 1 + rows - 1)

    def pair_copy(phase, h, i):
        return pltpu.make_async_remote_copy(
            src_ref=pair_send.at[phase, h, i], dst_ref=pair_recv.at[phase, h, i],
            send_sem=pair_ssem.at[phase, h, i], recv_sem=pair_rsem.at[phase, h, i],
            device_id={"col": sibling}, device_id_type=MESH,
        )

    def rs_refs(phase):
        return (logit_send, logit_recv) if phase == 0 else (resp_send.at[phase - 1], resp_recv.at[phase - 1])

    def rs_copy(phase, h, i):
        send, recv = rs_refs(phase)
        return pltpu.make_async_remote_copy(
            src_ref=send.at[h, i], dst_ref=recv.at[h, i],
            send_sem=rs_ssem.at[phase, h, i], recv_sem=rs_rsem.at[phase, h, i],
            device_id={"col": mine(i)}, device_id_type=MESH,
        )

    def start_reduce(phase, vector):
        vector = vector.astype(jnp.bfloat16)
        send = rs_refs(phase)[0]
        for h in range(PARTS):

            def one(u, carry):
                side, i = send_order(u)
                if phase == 0:
                    cov_copy(u, h).wait()
                part = lax.dot_general(
                    vector, cov[send_block(side, i), users(h)], (((1,), (1,)), ((), ())),
                    preferred_element_type=jnp.float32,
                )

                @pl.when(side == 0)
                def _():
                    pair_send[phase, h, i] = part
                    pair_copy(phase, h, i).start()

                @pl.when(side == 1)
                def _():
                    pair_copy(phase, h, i).wait_recv()
                    chip_sum[h] = part + pair_recv[phase, h, i]

                    @pl.when(i < chips - 1)
                    def _():
                        send[h, i] = chip_sum[h].astype(send.dtype)
                        rs_copy(phase, h, i).start()

                return carry

            lax.fori_loop(0, n, one, 0)

    def end_reduce(phase, h):
        recv = rs_refs(phase)[1]

        def add(i, total):
            rs_copy(phase, h, i).wait_recv()
            return total + recv[h, i].astype(jnp.float32)

        return lax.fori_loop(0, chips - 1, add, chip_sum[h])

    def ag_copy(phase, h, s):
        return pltpu.make_async_remote_copy(
            src_ref=got.at[phase, h, 0, 0], dst_ref=got.at[phase, h, 0, s],
            send_sem=ag_ssem.at[phase, h, s], recv_sem=ag_rsem.at[phase, h, s],
            device_id={"col": chip_after(s) * 2 + core}, device_id_type=MESH,
        )

    def forward(phase, h, s):
        return pltpu.make_async_remote_copy(
            src_ref=got.at[phase, h, 0, s], dst_ref=got.at[phase, h, 1, s],
            send_sem=pass_ssem.at[phase, h, s], recv_sem=pass_rsem.at[phase, h, s],
            device_id={"col": sibling}, device_id_type=MESH,
        )

    def give(phase, h, values):
        got[phase, h, 0, 0] = values
        forward(phase, h, 0).start()

        def send(s, carry):
            ag_copy(phase, h, s).start()
            return carry

        lax.fori_loop(1, chips, send, 0)

    def row_copy(phase, t, slot):
        return pltpu.make_async_remote_copy(
            src_ref=row_buf.at[phase, my_row], dst_ref=row_buf.at[phase, slot],
            send_sem=row_ssem.at[phase, t], recv_sem=row_rsem.at[phase, t],
            device_id={"row": lax.rem(my_row + t, rows)}, device_id_type=MESH,
        )

    def back_project(phase, meanwhile=None):
        total = jnp.zeros(weights_ref.shape, jnp.float32)
        for h in range(PARTS):

            def add(u, total):
                side, s = take_order(u)

                @pl.when(side == 1)
                def _():
                    forward(phase, h, s).wait_recv()

                @pl.when(jnp.logical_and(side == 0, s > 0))
                def _():
                    ag_copy(phase, h, s).wait_recv()
                    forward(phase, h, s).start()

                block = chip_before(s) * 2 + (1 - side) * core + side * (1 - core)
                return total + jnp.dot(
                    got[phase, h, side, s], cov[block, users(h)], preferred_element_type=jnp.float32
                )

            total = lax.fori_loop(0, n, add, total)
            if h == 0 and meanwhile is not None:
                meanwhile()
        row_buf[phase, my_row] = total

        def send_row(t, carry):
            row_copy(phase, t, my_row).start()
            return carry

        def wait_row(t, carry):
            row_copy(phase, t, lax.rem(my_row + rows - t, rows)).wait_recv()
            return carry

        lax.fori_loop(1, rows, send_row, 0)
        lax.fori_loop(1, rows, wait_row, 0)
        total = row_buf[phase, 0]
        for r in range(1, rows):
            total = total + row_buf[phase, r]
        return total

    def dot_copy(phase, j):
        return pltpu.make_async_remote_copy(
            src_ref=dot_send.at[phase], dst_ref=dot_recv.at[phase, j],
            send_sem=dot_ssem.at[phase, j], recv_sem=dot_rsem.at[phase, j],
            device_id={"col": target(j)}, device_id_type=MESH,
        )

    def send_dots(phase, *tiles):
        for k, tile in enumerate(tiles):
            dot_send[phase, k] = tile

        def send(j, carry):
            dot_copy(phase, j).start()
            return carry

        lax.fori_loop(1, n, send, 0)

    def take_dots(phase, tiles):
        def add(j, totals):
            dot_copy(phase, j).wait_recv()
            return tuple(total + dot_recv[phase, j, k] for k, total in enumerate(totals))

        totals = lax.fori_loop(1, n, add, tuple(dot_send[phase, k] for k in range(tiles)))
        return [jnp.sum(total, keepdims=True) for total in totals]

    def curve_copy(phase, t, slot):
        return pltpu.make_async_remote_copy(
            src_ref=curve_buf.at[phase, my_row], dst_ref=curve_buf.at[phase, slot],
            send_sem=curve_ssem.at[phase, t], recv_sem=curve_rsem.at[phase, t],
            device_id={"row": lax.rem(my_row + t, rows)}, device_id_type=MESH,
        )

    def send_curve(phase, tile):
        curve_buf[phase, my_row] = tile

        def send(t, carry):
            curve_copy(phase, t, my_row).start()
            return carry

        lax.fori_loop(1, rows, send, 0)

    def take_curve(phase):
        def wait(t, carry):
            curve_copy(phase, t, lax.rem(my_row + rows - t, rows)).wait_recv()
            return carry

        lax.fori_loop(1, rows, wait, 0)
        total = curve_buf[phase, 0]
        for r in range(1, rows):
            total = total + curve_buf[phase, r]
        return total

    weights = weights_ref[...]
    start_reduce(0, weights)
    shares, counted = [], []
    for h in range(PARTS):
        exponent = jnp.exp(end_reduce(0, h))
        shares.append(exponent / jnp.sum(exponent, axis=0, keepdims=True))
        label = labels_ref[:, h * half:(h + 1) * half]
        indicator = (label == lax.broadcasted_iota(jnp.int32, (classes, half), 0)).astype(jnp.float32)
        give(0, h, (shares[h] - indicator).astype(jnp.bfloat16))
        counted.append(count[:, h * half:(h + 1) * half] * shares[h])
    gradient = back_project(0) / user_total + RIDGE_WEIGHT * weights
    gradient_ref[...] = gradient

    residual = -gradient
    direction = residual
    newton_step = jnp.zeros_like(residual)
    norm_now = step_size = image = None
    residual_response, direction_response = [None] * PARTS, [None] * PARTS
    for iteration in range(ITERS):
        last = iteration + 1 == ITERS
        start_reduce(iteration + 1, direction if iteration == 0 else image)
        if iteration > 0:
            (norm_new,) = take_dots(2 * iteration - 1, 1)
            ratio = norm_new / norm_now
            direction = residual + ratio * direction
            norm_now = norm_new
        curve_tile = jnp.zeros((8, LANES), jnp.float32)
        for h in range(PARTS):
            response = end_reduce(iteration + 1, h)
            if iteration == 0:
                residual_response[h] = direction_response[h] = response
            else:
                residual_response[h] = residual_response[h] - step_size * response
                direction_response[h] = residual_response[h] + ratio * direction_response[h]
            centred = direction_response[h] - jnp.sum(shares[h] * direction_response[h], axis=0, keepdims=True)
            weighted = (counted[h] * centred).astype(jnp.bfloat16)
            if not last:
                give(iteration + 1, h, weighted)
            curve_tile = curve_tile + fold(weighted.astype(jnp.float32) * direction_response[h])
        send_curve(iteration, curve_tile)
        square = fold(direction * direction)

        def pass_curve():
            tiles = [take_curve(iteration) / sub_total + RIDGE_WEIGHT * square]
            send_dots(2 * iteration, *(tiles + [square] if iteration == 0 else tiles))

        if last:
            pass_curve()
        else:
            image = back_project(iteration + 1, pass_curve) / sub_total + RIDGE_WEIGHT * direction
        if iteration == 0:
            curve, norm_now = take_dots(0, 2)
        else:
            (curve,) = take_dots(2 * iteration, 1)
        step_size = norm_now / curve
        newton_step = newton_step + step_size * direction
        if not last:
            residual = residual - step_size * image
            send_dots(2 * iteration + 1, fold(residual * residual))
    step_ref[...] = newton_step

    def drain_chip(s, carry):
        for h in range(PARTS):
            for phase in range(ITERS + 1):
                pair_copy(phase, h, s).wait_send()
            for phase in range(ITERS):
                forward(phase, h, s).wait_send()

            @pl.when(s > 0)
            def _():
                for phase in range(ITERS + 1):
                    rs_copy(phase, h, s - 1).wait_send()
                for phase in range(ITERS):
                    ag_copy(phase, h, s).wait_send()

        return carry

    def drain_col(j, carry):
        for phase in range(2 * ITERS - 1):
            dot_copy(phase, j).wait_send()
        return carry

    def drain_row(t, carry):
        for phase in range(ITERS):
            row_copy(phase, t, my_row).wait_send()
            curve_copy(phase, t, my_row).wait_send()
        return carry

    lax.fori_loop(0, chips, drain_chip, 0)
    lax.fori_loop(1, n, drain_col, 0)
    lax.fori_loop(1, rows, drain_row, 0)


def body(covariates, labels, weights, sample_index):
    users, width = covariates.shape
    n, rows = lax.axis_size("col"), lax.axis_size("row")
    own, chips = users // n, n // 2
    half = own // PARTS
    classes = weights.shape[0]
    sub = sample_index.shape[0]
    dots = 2 * ITERS - 1
    dma = pltpu.SemaphoreType.DMA
    out = pl.pallas_call(
        functools.partial(kernel, n, rows, users * rows, sub * rows),
        out_shape=[jax.ShapeDtypeStruct((classes, width), jnp.float32)] * 2,
        in_specs=[pl.BlockSpec(memory_space=pltpu.HBM)] * 4,
        out_specs=[pl.BlockSpec(memory_space=pltpu.VMEM)] * 2,
        scratch_shapes=[
            pltpu.VMEM((n, own, width), jnp.bfloat16),
            pltpu.VMEM((1, own), jnp.int32),
            pltpu.VMEM((classes, width), jnp.float32),
            pltpu.VMEM((1, sub), jnp.int32),
            pltpu.VMEM((ITERS + 1, PARTS, chips, classes, half), jnp.float32),
            pltpu.VMEM((ITERS + 1, PARTS, chips, classes, half), jnp.float32),
            pltpu.VMEM((PARTS, chips, classes, half), jnp.float32),
            pltpu.VMEM((PARTS, chips, classes, half), jnp.float32),
            pltpu.VMEM((ITERS, PARTS, chips, classes, half), jnp.bfloat16),
            pltpu.VMEM((ITERS, PARTS, chips, classes, half), jnp.bfloat16),
            pltpu.VMEM((PARTS, classes, half), jnp.float32),
            pltpu.VMEM((ITERS, PARTS, 2, chips, classes, half), jnp.bfloat16),
            pltpu.VMEM((ITERS, rows, classes, width), jnp.float32),
            pltpu.VMEM((ITERS, rows, 8, LANES), jnp.float32),
            pltpu.VMEM((dots, 2, 8, LANES), jnp.float32),
            pltpu.VMEM((dots, n, 2, 8, LANES), jnp.float32),
            dma((PARTS, n)), dma((3,)),
            dma((ITERS + 1, PARTS, chips)), dma((ITERS + 1, PARTS, chips)),
            dma((ITERS + 1, PARTS, chips)), dma((ITERS + 1, PARTS, chips)),
            dma((ITERS, PARTS, chips)), dma((ITERS, PARTS, chips)),
            dma((ITERS, PARTS, chips)), dma((ITERS, PARTS, chips)),
            dma((ITERS, rows)), dma((ITERS, rows)),
            dma((ITERS, rows)), dma((ITERS, rows)),
            dma((dots, n)), dma((dots, n)),
        ],
        compiler_params=pltpu.CompilerParams(
            collective_id=0, has_side_effects=True, vmem_limit_bytes=60 * 1024 * 1024
        ),
        name="newton_step",
    )(
        covariates.reshape(n, own, width), labels.reshape(n, 1, own), weights, sample_index.reshape(1, sub)
    )
    return tuple(out)


def solution(mesh):
    in_specs = (P("row", "col"), P("row"), P(None, "col"), P("row"))
    out_specs = (P(None, "col"), P(None, "col"))
    return jax.shard_map(body, mesh=mesh, in_specs=in_specs, out_specs=out_specs, check_vma=False)
```

```python
import functools

import jax
import jax.numpy as jnp
from jax import lax
from jax.experimental import pallas as pl
from jax.experimental.pallas import tpu as pltpu
from jax.sharding import PartitionSpec as P

ITERS = 2
RIDGE_WEIGHT = 0.004
LANES = 128
MESH = pl.DeviceIdType.MESH


def fold(value):
    value = value[:8] + value[8:]
    total = value[:, :LANES]
    for start in range(LANES, value.shape[1], LANES):
        total = total + value[:, start:start + LANES]
    return total


def kernel(
    n, rows, user_total, sub_total,
    cov_hbm, labels_hbm, weights_hbm, index_hbm, gradient_ref, step_ref,
    cov, labels_ref, weights_ref, index_ref, pair_send, pair_recv, logit_send, logit_recv, resp_send, resp_recv,
    chip_sum, got, row_buf, curve_buf, dot_send, dot_recv,
    cov_sem, small_sem, pair_ssem, pair_rsem, rs_ssem, rs_rsem, ag_ssem, ag_rsem, pass_ssem, pass_rsem,
    row_ssem, row_rsem, curve_ssem, curve_rsem, dot_ssem, dot_rsem,
):
    me = lax.axis_index("col")
    my_row = lax.axis_index("row")
    chips = n // 2
    pairs, own = cov.shape[1], cov.shape[2] // 2
    classes = weights_ref.shape[0]

    chip, core = me // 2, lax.rem(me, 2)
    sibling = chip * 2 + 1 - core
    own_block = core * chips + chip

    def target(j):
        return lax.rem(me + j, n)

    def chip_after(s):
        return lax.rem(chip + s, chips)

    def chip_before(s):
        return lax.rem(chip + chips - s, chips)

    def send_order(u):
        side, i = u // pairs, lax.rem(u, pairs)
        return side, i, lax.rem(chip // 2 + i + 1, pairs)

    def half_of(side):
        return side * core + (1 - side) * (1 - core)

    def cov_copy(u):
        side, i, pair = send_order(u)
        half = half_of(side)
        return pltpu.make_async_copy(cov_hbm.at[half, pair], cov.at[half, pair], cov_sem.at[u])

    small_copies = [
        pltpu.make_async_copy(weights_hbm, weights_ref, small_sem.at[0]),
        pltpu.make_async_copy(index_hbm, index_ref, small_sem.at[1]),
        pltpu.make_async_copy(labels_hbm.at[own_block], labels_ref, small_sem.at[2]),
    ]
    for copy in small_copies:
        copy.start()

    def start_cov(u, carry):
        cov_copy(u).start()
        return carry

    lax.fori_loop(0, 2 * pairs, start_cov, 0)

    barrier = pltpu.get_barrier_semaphore()

    def greet_col(j, carry):
        pl.semaphore_signal(barrier, inc=1, device_id={"col": target(j)}, device_id_type=MESH)
        return carry

    def greet_row(t, carry):
        pl.semaphore_signal(
            barrier, inc=1, device_id={"row": lax.rem(my_row + t, rows)}, device_id_type=MESH
        )
        return carry

    lax.fori_loop(1, n, greet_col, 0)
    lax.fori_loop(1, rows, greet_row, 0)

    for copy in small_copies:
        copy.wait()

    groups = own // LANES
    padded = max(16, groups)
    within = index_ref[...] - my_row * (n * own) - own_block * own
    lane = jnp.bitwise_and(within, LANES - 1)
    group = jnp.right_shift(within - lane, 7)
    group_hot = (lax.broadcasted_iota(jnp.int32, (padded, within.shape[1]), 0) == group)
    lane_hot = (lax.broadcasted_iota(jnp.int32, (LANES, within.shape[1]), 0) == lane)
    counts = lax.dot_general(
        group_hot.astype(jnp.float32).astype(jnp.bfloat16), lane_hot.astype(jnp.float32).astype(jnp.bfloat16),
        (((1,), (1,)), ((), ())), preferred_element_type=jnp.float32,
    )
    count = jnp.concatenate([counts[g:g + 1] for g in range(groups)], axis=1)

    pl.semaphore_wait(barrier, n - 1 + rows - 1)

    def pair_copy(phase, i):
        return pltpu.make_async_remote_copy(
            src_ref=pair_send.at[phase, i], dst_ref=pair_recv.at[phase, i],
            send_sem=pair_ssem.at[phase, i], recv_sem=pair_rsem.at[phase, i],
            device_id={"col": sibling}, device_id_type=MESH,
        )

    def rs_copy(phase, send, recv, to, slot):
        return pltpu.make_async_remote_copy(
            src_ref=send.at[to], dst_ref=recv.at[slot],
            send_sem=rs_ssem.at[phase, to], recv_sem=rs_rsem.at[phase, slot],
            device_id={"col": to * 2 + core}, device_id_type=MESH,
        )

    def reduce_users(phase, vector, send, recv):
        vector = vector.astype(jnp.bfloat16)

        def one(u, carry):
            side, i, pair = send_order(u)
            if phase == 0:
                cov_copy(u).wait()
            part = lax.dot_general(
                vector, cov[half_of(side), pair], (((1,), (1,)), ((), ())), preferred_element_type=jnp.float32
            )

            @pl.when(side == 0)
            def _():
                pair_send[phase, i] = part
                pair_copy(phase, i).start()

            @pl.when(side == 1)
            def _():
                pair_copy(phase, i).wait_recv()
                both = part + pair_recv[phase, i]
                for h in range(2):
                    to = pair * 2 + h
                    value = both[:, h * own:(h + 1) * own]

                    @pl.when(to != chip)
                    def _():
                        send[to] = value.astype(send.dtype)
                        rs_copy(phase, send, recv, to, chip).start()

                    @pl.when(to == chip)
                    def _():
                        chip_sum[...] = value

            return carry

        lax.fori_loop(0, 2 * pairs, one, 0)

        def add(s, total):
            origin = chip_before(s)
            rs_copy(phase, send, recv, origin, origin).wait_recv()
            return total + recv[origin].astype(jnp.float32)

        return lax.fori_loop(1, chips, add, chip_sum[...])

    def ag_copy(phase, to, slot):
        return pltpu.make_async_remote_copy(
            src_ref=got.at[phase, 0, chip], dst_ref=got.at[phase, 0, slot],
            send_sem=ag_ssem.at[phase, to], recv_sem=ag_rsem.at[phase, slot],
            device_id={"col": to * 2 + core}, device_id_type=MESH,
        )

    def forward(phase, origin):
        return pltpu.make_async_remote_copy(
            src_ref=got.at[phase, 0, origin], dst_ref=got.at[phase, 1, origin],
            send_sem=pass_ssem.at[phase, origin], recv_sem=pass_rsem.at[phase, origin],
            device_id={"col": sibling}, device_id_type=MESH,
        )

    def row_copy(phase, t, slot):
        return pltpu.make_async_remote_copy(
            src_ref=row_buf.at[phase, my_row], dst_ref=row_buf.at[phase, slot],
            send_sem=row_ssem.at[phase, t], recv_sem=row_rsem.at[phase, t],
            device_id={"row": lax.rem(my_row + t, rows)}, device_id_type=MESH,
        )

    def back_project(phase, values, meanwhile=None):
        got[phase, 0, chip] = values
        forward(phase, chip).start()

        def send(s, carry):
            ag_copy(phase, chip_after(s), chip).start()
            return carry

        lax.fori_loop(1, chips, send, 0)

        def term(side, pair):
            both = jnp.concatenate([got[phase, side, pair * 2], got[phase, side, pair * 2 + 1]], axis=1)
            return jnp.dot(
                both, cov[(1 - side) * core + side * (1 - core), pair], preferred_element_type=jnp.float32
            )

        def direct(q, total):
            pair = lax.rem(chip // 2 + q, pairs)
            for h in range(2):
                origin = pair * 2 + h

                @pl.when(origin != chip)
                def _():
                    ag_copy(phase, origin, origin).wait_recv()
                    forward(phase, origin).start()

            return total + term(0, pair)

        def passed(q, total):
            pair = lax.rem(chip // 2 + q, pairs)
            for h in range(2):
                forward(phase, pair * 2 + h).wait_recv()
            return total + term(1, pair)

        total = lax.fori_loop(0, pairs, direct, jnp.zeros(weights_ref.shape, jnp.float32))
        if meanwhile is not None:
            meanwhile()
        row_buf[phase, my_row] = lax.fori_loop(0, pairs, passed, total)

        def send_row(t, carry):
            row_copy(phase, t, my_row).start()
            return carry

        def wait_row(t, carry):
            row_copy(phase, t, lax.rem(my_row + rows - t, rows)).wait_recv()
            return carry

        lax.fori_loop(1, rows, send_row, 0)
        lax.fori_loop(1, rows, wait_row, 0)
        total = row_buf[phase, 0]
        for r in range(1, rows):
            total = total + row_buf[phase, r]
        return total

    def dot_copy(phase, j):
        return pltpu.make_async_remote_copy(
            src_ref=dot_send.at[phase], dst_ref=dot_recv.at[phase, j],
            send_sem=dot_ssem.at[phase, j], recv_sem=dot_rsem.at[phase, j],
            device_id={"col": target(j)}, device_id_type=MESH,
        )

    def send_dots(phase, *tiles):
        for k, tile in enumerate(tiles):
            dot_send[phase, k] = tile

        def send(j, carry):
            dot_copy(phase, j).start()
            return carry

        lax.fori_loop(1, n, send, 0)

    def take_dots(phase, tiles):
        def add(j, totals):
            dot_copy(phase, j).wait_recv()
            return tuple(total + dot_recv[phase, j, k] for k, total in enumerate(totals))

        totals = lax.fori_loop(1, n, add, tuple(dot_send[phase, k] for k in range(tiles)))
        return [jnp.sum(total, keepdims=True) for total in totals]

    def curve_copy(phase, t, slot):
        return pltpu.make_async_remote_copy(
            src_ref=curve_buf.at[phase, my_row], dst_ref=curve_buf.at[phase, slot],
            send_sem=curve_ssem.at[phase, t], recv_sem=curve_rsem.at[phase, t],
            device_id={"row": lax.rem(my_row + t, rows)}, device_id_type=MESH,
        )

    def send_curve(phase, tile):
        curve_buf[phase, my_row] = tile

        def send(t, carry):
            curve_copy(phase, t, my_row).start()
            return carry

        lax.fori_loop(1, rows, send, 0)

    def take_curve(phase):
        def wait(t, carry):
            curve_copy(phase, t, lax.rem(my_row + rows - t, rows)).wait_recv()
            return carry

        lax.fori_loop(1, rows, wait, 0)
        total = curve_buf[phase, 0]
        for r in range(1, rows):
            total = total + curve_buf[phase, r]
        return total

    weights = weights_ref[...]
    logits = reduce_users(0, weights, logit_send, logit_recv)
    exponent = jnp.exp(logits)
    shares = exponent / jnp.sum(exponent, axis=0, keepdims=True)
    label = labels_ref[...]
    indicator = (label == lax.broadcasted_iota(jnp.int32, (classes, own), 0)).astype(jnp.float32)
    misfit = (shares - indicator).astype(jnp.bfloat16)
    gradient = back_project(0, misfit) / user_total + RIDGE_WEIGHT * weights
    gradient_ref[...] = gradient
    counted = count * shares

    residual = -gradient
    direction = residual
    newton_step = jnp.zeros_like(residual)
    norm_now = step_size = image = residual_response = direction_response = None
    for iteration in range(ITERS):
        last = iteration + 1 == ITERS
        vector = direction if iteration == 0 else image
        response = reduce_users(
            iteration + 1, vector, resp_send.at[iteration], resp_recv.at[iteration]
        )
        if iteration == 0:
            residual_response = direction_response = response
        else:
            (norm_new,) = take_dots(2 * iteration - 1, 1)
            ratio = norm_new / norm_now
            direction = residual + ratio * direction
            norm_now = norm_new
            residual_response = residual_response - step_size * response
            direction_response = residual_response + ratio * direction_response
        centred = direction_response - jnp.sum(shares * direction_response, axis=0, keepdims=True)
        weighted = (counted * centred).astype(jnp.bfloat16)
        send_curve(iteration, fold(weighted.astype(jnp.float32) * direction_response))
        square = fold(direction * direction)

        def pass_curve():
            tiles = [take_curve(iteration) / sub_total + RIDGE_WEIGHT * square]
            send_dots(2 * iteration, *(tiles + [square] if iteration == 0 else tiles))

        if last:
            pass_curve()
        else:
            image = back_project(iteration + 1, weighted, pass_curve) / sub_total + RIDGE_WEIGHT * direction
        if iteration == 0:
            curve, norm_now = take_dots(0, 2)
        else:
            (curve,) = take_dots(2 * iteration, 1)
        step_size = norm_now / curve
        newton_step = newton_step + step_size * direction
        if not last:
            residual = residual - step_size * image
            send_dots(2 * iteration + 1, fold(residual * residual))
    step_ref[...] = newton_step

    def drain_pair(i, carry):
        for phase in range(ITERS + 1):
            pair_copy(phase, i).wait_send()
        return carry

    def drain_chip(s, carry):
        to = chip_after(s)
        rs_copy(0, logit_send, logit_recv, to, chip).wait_send()
        for phase in range(ITERS):
            rs_copy(phase + 1, resp_send.at[phase], resp_recv.at[phase], to, chip).wait_send()
            ag_copy(phase, to, chip).wait_send()
            forward(phase, to).wait_send()
        return carry

    def drain_col(j, carry):
        for phase in range(2 * ITERS - 1):
            dot_copy(phase, j).wait_send()
        return carry

    def drain_row(t, carry):
        for phase in range(ITERS):
            row_copy(phase, t, my_row).wait_send()
            curve_copy(phase, t, my_row).wait_send()
        return carry

    for phase in range(ITERS):
        forward(phase, chip).wait_send()
    lax.fori_loop(0, pairs, drain_pair, 0)
    lax.fori_loop(1, chips, drain_chip, 0)
    lax.fori_loop(1, n, drain_col, 0)
    lax.fori_loop(1, rows, drain_row, 0)


def body(covariates, labels, weights, sample_index):
    users, width = covariates.shape
    n, rows = lax.axis_size("col"), lax.axis_size("row")
    own, chips, pairs = users // n, n // 2, n // 4
    classes = weights.shape[0]
    sub = sample_index.shape[0]
    dots = 2 * ITERS - 1
    dma = pltpu.SemaphoreType.DMA
    out = pl.pallas_call(
        functools.partial(kernel, n, rows, users * rows, sub * rows),
        out_shape=[jax.ShapeDtypeStruct((classes, width), jnp.float32)] * 2,
        in_specs=[pl.BlockSpec(memory_space=pltpu.HBM)] * 4,
        out_specs=[pl.BlockSpec(memory_space=pltpu.VMEM)] * 2,
        scratch_shapes=[
            pltpu.VMEM((2, pairs, 2 * own, width), jnp.bfloat16),
            pltpu.VMEM((1, own), jnp.int32),
            pltpu.VMEM((classes, width), jnp.float32),
            pltpu.VMEM((1, sub), jnp.int32),
            pltpu.VMEM((ITERS + 1, pairs, classes, 2 * own), jnp.float32),
            pltpu.VMEM((ITERS + 1, pairs, classes, 2 * own), jnp.float32),
            pltpu.VMEM((chips, classes, own), jnp.float32),
            pltpu.VMEM((chips, classes, own), jnp.float32),
            pltpu.VMEM((ITERS, chips, classes, own), jnp.bfloat16),
            pltpu.VMEM((ITERS, chips, classes, own), jnp.bfloat16),
            pltpu.VMEM((classes, own), jnp.float32),
            pltpu.VMEM((ITERS, 2, chips, classes, own), jnp.bfloat16),
            pltpu.VMEM((ITERS, rows, classes, width), jnp.float32),
            pltpu.VMEM((ITERS, rows, 8, LANES), jnp.float32),
            pltpu.VMEM((dots, 2, 8, LANES), jnp.float32),
            pltpu.VMEM((dots, n, 2, 8, LANES), jnp.float32),
            dma((n,)), dma((3,)),
            dma((ITERS + 1, pairs)), dma((ITERS + 1, pairs)),
            dma((ITERS + 1, chips)), dma((ITERS + 1, chips)),
            dma((ITERS, chips)), dma((ITERS, chips)),
            dma((ITERS, chips)), dma((ITERS, chips)),
            dma((ITERS, rows)), dma((ITERS, rows)),
            dma((ITERS, rows)), dma((ITERS, rows)),
            dma((dots, n)), dma((dots, n)),
        ],
        compiler_params=pltpu.CompilerParams(
            collective_id=0, has_side_effects=True, vmem_limit_bytes=60 * 1024 * 1024
        ),
        name="newton_step",
    )(
        covariates.reshape(2, pairs, 2 * own, width), labels.reshape(n, 1, own), weights, sample_index.reshape(1, sub)
    )
    return tuple(out)


def solution(mesh):
    in_specs = (P("row", "col"), P("row"), P(None, "col"), P("row"))
    out_specs = (P(None, "col"), P(None, "col"))
    return jax.shard_map(body, mesh=mesh, in_specs=in_specs, out_specs=out_specs, check_vma=False)
```

```python
import functools

import jax
import jax.numpy as jnp
from jax import lax
from jax.experimental import pallas as pl
from jax.experimental.pallas import tpu as pltpu
from jax.sharding import PartitionSpec as P

ITERS = 2
RIDGE_WEIGHT = 0.004
LANES = 128
MESH = pl.DeviceIdType.MESH


def fold(value):
    value = value[:8] + value[8:]
    total = value[:, :LANES]
    for start in range(LANES, value.shape[1], LANES):
        total = total + value[:, start:start + LANES]
    return total


def kernel(
    n, rows, user_total, sub_total,
    cov_hbm, labels_hbm, weights_hbm, index_hbm, gradient_ref, step_ref,
    cov, labels_ref, weights_ref, index_ref, pair_send, pair_recv, logit_send, logit_recv, resp_send, resp_recv,
    chip_sum, got, row_buf, curve_buf, dot_send, dot_recv,
    cov_sem, small_sem, pair_ssem, pair_rsem, rs_ssem, rs_rsem, ag_ssem, ag_rsem, pass_ssem, pass_rsem,
    row_ssem, row_rsem, curve_ssem, curve_rsem, dot_ssem, dot_rsem,
):
    me = lax.axis_index("col")
    my_row = lax.axis_index("row")
    chips = n // 2
    pairs, own = cov.shape[1], cov.shape[2] // 2
    classes = weights_ref.shape[0]

    chip, core = me // 2, lax.rem(me, 2)
    sibling = chip * 2 + 1 - core
    own_block = core * chips + chip

    def target(j):
        return lax.rem(me + j, n)

    def chip_after(s):
        return lax.rem(chip + s, chips)

    def chip_before(s):
        return lax.rem(chip + chips - s, chips)

    def send_order(u):
        side, i = u // pairs, lax.rem(u, pairs)
        return side, i, lax.rem(chip // 2 + i + 1, pairs)

    def half_of(side):
        return side * core + (1 - side) * (1 - core)

    def cov_copy(u):
        side, i, pair = send_order(u)
        half = half_of(side)
        return pltpu.make_async_copy(cov_hbm.at[half, pair], cov.at[half, pair], cov_sem.at[u])

    small_copies = [
        pltpu.make_async_copy(weights_hbm, weights_ref, small_sem.at[0]),
        pltpu.make_async_copy(index_hbm, index_ref, small_sem.at[1]),
        pltpu.make_async_copy(labels_hbm.at[own_block], labels_ref, small_sem.at[2]),
    ]
    for copy in small_copies:
        copy.start()

    def start_cov(u, carry):
        cov_copy(u).start()
        return carry

    lax.fori_loop(0, 2 * pairs, start_cov, 0)

    barrier = pltpu.get_barrier_semaphore()

    def greet_col(j, carry):
        pl.semaphore_signal(barrier, inc=1, device_id={"col": target(j)}, device_id_type=MESH)
        return carry

    def greet_row(t, carry):
        pl.semaphore_signal(
            barrier, inc=1, device_id={"row": lax.rem(my_row + t, rows)}, device_id_type=MESH
        )
        return carry

    lax.fori_loop(1, n, greet_col, 0)
    lax.fori_loop(1, rows, greet_row, 0)

    pl.semaphore_wait(barrier, n - 1 + rows - 1)

    def count_users():
        small_copies[1].wait()
        groups = own // LANES
        padded = max(16, groups)
        within = index_ref[...] - my_row * (n * own) - own_block * own
        lane = jnp.bitwise_and(within, LANES - 1)
        group = jnp.right_shift(within - lane, 7)
        group_hot = (lax.broadcasted_iota(jnp.int32, (padded, within.shape[1]), 0) == group)
        lane_hot = (lax.broadcasted_iota(jnp.int32, (LANES, within.shape[1]), 0) == lane)
        counts = lax.dot_general(
            group_hot.astype(jnp.float32).astype(jnp.bfloat16), lane_hot.astype(jnp.float32).astype(jnp.bfloat16),
            (((1,), (1,)), ((), ())), preferred_element_type=jnp.float32,
        )
        return jnp.concatenate([counts[g:g + 1] for g in range(groups)], axis=1)

    def pair_copy(phase, i):
        return pltpu.make_async_remote_copy(
            src_ref=pair_send.at[phase, i], dst_ref=pair_recv.at[phase, i],
            send_sem=pair_ssem.at[phase, i], recv_sem=pair_rsem.at[phase, i],
            device_id={"col": sibling}, device_id_type=MESH,
        )

    def rs_copy(phase, send, recv, to, slot):
        return pltpu.make_async_remote_copy(
            src_ref=send.at[to], dst_ref=recv.at[slot],
            send_sem=rs_ssem.at[phase, to], recv_sem=rs_rsem.at[phase, slot],
            device_id={"col": to * 2 + core}, device_id_type=MESH,
        )

    def reduce_users(phase, vector, send, recv):
        vector = vector.astype(jnp.bfloat16)

        def one(u, carry):
            side, i, pair = send_order(u)
            if phase == 0:
                cov_copy(u).wait()
            part = lax.dot_general(
                vector, cov[half_of(side), pair], (((1,), (1,)), ((), ())), preferred_element_type=jnp.float32
            )

            @pl.when(side == 0)
            def _():
                pair_send[phase, i] = part
                pair_copy(phase, i).start()

            @pl.when(side == 1)
            def _():
                pair_copy(phase, i).wait_recv()
                both = part + pair_recv[phase, i]
                for h in range(2):
                    to = pair * 2 + h
                    value = both[:, h * own:(h + 1) * own]

                    @pl.when(to != chip)
                    def _():
                        send[to] = value.astype(send.dtype)
                        rs_copy(phase, send, recv, to, chip).start()

                    @pl.when(to == chip)
                    def _():
                        chip_sum[...] = value

            return carry

        lax.fori_loop(0, 2 * pairs, one, 0)

        def add(s, total):
            origin = chip_before(s)
            rs_copy(phase, send, recv, origin, origin).wait_recv()
            return total + recv[origin].astype(jnp.float32)

        return lax.fori_loop(1, chips, add, chip_sum[...])

    def ag_copy(phase, to, slot):
        return pltpu.make_async_remote_copy(
            src_ref=got.at[phase, 0, chip], dst_ref=got.at[phase, 0, slot],
            send_sem=ag_ssem.at[phase, to], recv_sem=ag_rsem.at[phase, slot],
            device_id={"col": to * 2 + core}, device_id_type=MESH,
        )

    def forward(phase, origin):
        return pltpu.make_async_remote_copy(
            src_ref=got.at[phase, 0, origin], dst_ref=got.at[phase, 1, origin],
            send_sem=pass_ssem.at[phase, origin], recv_sem=pass_rsem.at[phase, origin],
            device_id={"col": sibling}, device_id_type=MESH,
        )

    def row_copy(phase, t, slot):
        return pltpu.make_async_remote_copy(
            src_ref=row_buf.at[phase, my_row], dst_ref=row_buf.at[phase, slot],
            send_sem=row_ssem.at[phase, t], recv_sem=row_rsem.at[phase, t],
            device_id={"row": lax.rem(my_row + t, rows)}, device_id_type=MESH,
        )

    def back_project(phase, values, meanwhile=None, beside=None):
        got[phase, 0, chip] = values
        forward(phase, chip).start()

        def send(s, carry):
            ag_copy(phase, chip_after(s), chip).start()
            return carry

        lax.fori_loop(1, chips, send, 0)

        if beside is not None:
            beside()

        def term(side, pair):
            both = jnp.concatenate([got[phase, side, pair * 2], got[phase, side, pair * 2 + 1]], axis=1)
            return jnp.dot(
                both, cov[(1 - side) * core + side * (1 - core), pair], preferred_element_type=jnp.float32
            )

        def direct(q, total):
            pair = lax.rem(chip // 2 + q, pairs)
            for h in range(2):
                origin = pair * 2 + h

                @pl.when(origin != chip)
                def _():
                    ag_copy(phase, origin, origin).wait_recv()
                    forward(phase, origin).start()

            return total + term(0, pair)

        def passed(q, total):
            pair = lax.rem(chip // 2 + q, pairs)
            for h in range(2):
                forward(phase, pair * 2 + h).wait_recv()
            return total + term(1, pair)

        total = lax.fori_loop(0, pairs, direct, jnp.zeros(weights_ref.shape, jnp.float32))
        if meanwhile is not None:
            meanwhile()
        row_buf[phase, my_row] = lax.fori_loop(0, pairs, passed, total)

        def send_row(t, carry):
            row_copy(phase, t, my_row).start()
            return carry

        def wait_row(t, carry):
            row_copy(phase, t, lax.rem(my_row + rows - t, rows)).wait_recv()
            return carry

        lax.fori_loop(1, rows, send_row, 0)
        lax.fori_loop(1, rows, wait_row, 0)
        total = row_buf[phase, 0]
        for r in range(1, rows):
            total = total + row_buf[phase, r]
        return total

    def dot_copy(phase, j):
        return pltpu.make_async_remote_copy(
            src_ref=dot_send.at[phase], dst_ref=dot_recv.at[phase, j],
            send_sem=dot_ssem.at[phase, j], recv_sem=dot_rsem.at[phase, j],
            device_id={"col": target(j)}, device_id_type=MESH,
        )

    def send_dots(phase, *tiles):
        for k, tile in enumerate(tiles):
            dot_send[phase, k] = tile

        def send(j, carry):
            dot_copy(phase, j).start()
            return carry

        lax.fori_loop(1, n, send, 0)

    def take_dots(phase, tiles):
        def add(j, totals):
            dot_copy(phase, j).wait_recv()
            return tuple(total + dot_recv[phase, j, k] for k, total in enumerate(totals))

        totals = lax.fori_loop(1, n, add, tuple(dot_send[phase, k] for k in range(tiles)))
        return [jnp.sum(total, keepdims=True) for total in totals]

    def curve_copy(phase, t, slot):
        return pltpu.make_async_remote_copy(
            src_ref=curve_buf.at[phase, my_row], dst_ref=curve_buf.at[phase, slot],
            send_sem=curve_ssem.at[phase, t], recv_sem=curve_rsem.at[phase, t],
            device_id={"row": lax.rem(my_row + t, rows)}, device_id_type=MESH,
        )

    def send_curve(phase, tile):
        curve_buf[phase, my_row] = tile

        def send(t, carry):
            curve_copy(phase, t, my_row).start()
            return carry

        lax.fori_loop(1, rows, send, 0)

    def take_curve(phase):
        def wait(t, carry):
            curve_copy(phase, t, lax.rem(my_row + rows - t, rows)).wait_recv()
            return carry

        lax.fori_loop(1, rows, wait, 0)
        total = curve_buf[phase, 0]
        for r in range(1, rows):
            total = total + curve_buf[phase, r]
        return total

    small_copies[0].wait()
    weights = weights_ref[...]
    logits = reduce_users(0, weights, logit_send, logit_recv)
    exponent = jnp.exp(logits)
    shares = exponent / jnp.sum(exponent, axis=0, keepdims=True)
    small_copies[2].wait()
    label = labels_ref[...]
    indicator = (label == lax.broadcasted_iota(jnp.int32, (classes, own), 0)).astype(jnp.float32)
    misfit = (shares - indicator).astype(jnp.bfloat16)
    counts = []
    gradient = back_project(0, misfit, beside=lambda: counts.append(count_users())) / user_total + RIDGE_WEIGHT * weights
    gradient_ref[...] = gradient
    counted = counts[0] * shares

    residual = -gradient
    direction = residual
    newton_step = jnp.zeros_like(residual)
    norm_now = step_size = image = residual_response = direction_response = None
    for iteration in range(ITERS):
        last = iteration + 1 == ITERS
        vector = direction if iteration == 0 else image
        response = reduce_users(
            iteration + 1, vector, resp_send.at[iteration], resp_recv.at[iteration]
        )
        if iteration == 0:
            residual_response = direction_response = response
        else:
            (norm_new,) = take_dots(2 * iteration - 1, 1)
            ratio = norm_new / norm_now
            direction = residual + ratio * direction
            norm_now = norm_new
            residual_response = residual_response - step_size * response
            direction_response = residual_response + ratio * direction_response
        centred = direction_response - jnp.sum(shares * direction_response, axis=0, keepdims=True)
        weighted = (counted * centred).astype(jnp.bfloat16)
        send_curve(iteration, fold(weighted.astype(jnp.float32) * direction_response))
        square = fold(direction * direction)

        def pass_curve():
            tiles = [take_curve(iteration) / sub_total + RIDGE_WEIGHT * square]
            send_dots(2 * iteration, *(tiles + [square] if iteration == 0 else tiles))

        if last:
            pass_curve()
        else:
            image = back_project(iteration + 1, weighted, pass_curve) / sub_total + RIDGE_WEIGHT * direction
        if iteration == 0:
            curve, norm_now = take_dots(0, 2)
        else:
            (curve,) = take_dots(2 * iteration, 1)
        step_size = norm_now / curve
        newton_step = newton_step + step_size * direction
        if not last:
            residual = residual - step_size * image
            send_dots(2 * iteration + 1, fold(residual * residual))
    step_ref[...] = newton_step

    def drain_pair(i, carry):
        for phase in range(ITERS + 1):
            pair_copy(phase, i).wait_send()
        return carry

    def drain_chip(s, carry):
        to = chip_after(s)
        rs_copy(0, logit_send, logit_recv, to, chip).wait_send()
        for phase in range(ITERS):
            rs_copy(phase + 1, resp_send.at[phase], resp_recv.at[phase], to, chip).wait_send()
            ag_copy(phase, to, chip).wait_send()
            forward(phase, to).wait_send()
        return carry

    def drain_col(j, carry):
        for phase in range(2 * ITERS - 1):
            dot_copy(phase, j).wait_send()
        return carry

    def drain_row(t, carry):
        for phase in range(ITERS):
            row_copy(phase, t, my_row).wait_send()
            curve_copy(phase, t, my_row).wait_send()
        return carry

    for phase in range(ITERS):
        forward(phase, chip).wait_send()
    lax.fori_loop(0, pairs, drain_pair, 0)
    lax.fori_loop(1, chips, drain_chip, 0)
    lax.fori_loop(1, n, drain_col, 0)
    lax.fori_loop(1, rows, drain_row, 0)


def body(covariates, labels, weights, sample_index):
    users, width = covariates.shape
    n, rows = lax.axis_size("col"), lax.axis_size("row")
    own, chips, pairs = users // n, n // 2, n // 4
    classes = weights.shape[0]
    sub = sample_index.shape[0]
    dots = 2 * ITERS - 1
    dma = pltpu.SemaphoreType.DMA
    out = pl.pallas_call(
        functools.partial(kernel, n, rows, users * rows, sub * rows),
        out_shape=[jax.ShapeDtypeStruct((classes, width), jnp.float32)] * 2,
        in_specs=[pl.BlockSpec(memory_space=pltpu.HBM)] * 4,
        out_specs=[pl.BlockSpec(memory_space=pltpu.VMEM)] * 2,
        scratch_shapes=[
            pltpu.VMEM((2, pairs, 2 * own, width), jnp.bfloat16),
            pltpu.VMEM((1, own), jnp.int32),
            pltpu.VMEM((classes, width), jnp.float32),
            pltpu.VMEM((1, sub), jnp.int32),
            pltpu.VMEM((ITERS + 1, pairs, classes, 2 * own), jnp.float32),
            pltpu.VMEM((ITERS + 1, pairs, classes, 2 * own), jnp.float32),
            pltpu.VMEM((chips, classes, own), jnp.float32),
            pltpu.VMEM((chips, classes, own), jnp.float32),
            pltpu.VMEM((ITERS, chips, classes, own), jnp.bfloat16),
            pltpu.VMEM((ITERS, chips, classes, own), jnp.bfloat16),
            pltpu.VMEM((classes, own), jnp.float32),
            pltpu.VMEM((ITERS, 2, chips, classes, own), jnp.bfloat16),
            pltpu.VMEM((ITERS, rows, classes, width), jnp.float32),
            pltpu.VMEM((ITERS, rows, 8, LANES), jnp.float32),
            pltpu.VMEM((dots, 2, 8, LANES), jnp.float32),
            pltpu.VMEM((dots, n, 2, 8, LANES), jnp.float32),
            dma((n,)), dma((3,)),
            dma((ITERS + 1, pairs)), dma((ITERS + 1, pairs)),
            dma((ITERS + 1, chips)), dma((ITERS + 1, chips)),
            dma((ITERS, chips)), dma((ITERS, chips)),
            dma((ITERS, chips)), dma((ITERS, chips)),
            dma((ITERS, rows)), dma((ITERS, rows)),
            dma((ITERS, rows)), dma((ITERS, rows)),
            dma((dots, n)), dma((dots, n)),
        ],
        compiler_params=pltpu.CompilerParams(
            collective_id=0, has_side_effects=True, vmem_limit_bytes=60 * 1024 * 1024
        ),
        name="newton_step",
    )(
        covariates.reshape(2, pairs, 2 * own, width), labels.reshape(n, 1, own), weights, sample_index.reshape(1, sub)
    )
    return tuple(out)


def solution(mesh):
    in_specs = (P("row", "col"), P("row"), P(None, "col"), P("row"))
    out_specs = (P(None, "col"), P(None, "col"))
    return jax.shard_map(body, mesh=mesh, in_specs=in_specs, out_specs=out_specs, check_vma=False)
```
